32 devices in a mesh: ctx: 8 (over z, x), ch: 2 (over y), dp: 2 (over core).
Axes of the slice: x: 2, y: 2, z: 4, core: 2. Of those that a mesh axis runs over, the one named last changes fastest.
Arguments:
- raw_streams: bfloat16 [16384, 3, 256], P(('dp', 'ctx'), None, 'ch'), parts along dimension 0, may hold values from -6 to 6
- short_taps: float32 [7, 3, 256], P(None, None, 'ch'), may hold values from -2.4 to 2.4
- decay_rate: float32 [16, 16], P('ch'), may hold values from 1.2207031e-06 to 0.08
- residue: float32 [16, 16], P('ch'), may hold values from -2 to 2
- medium_filter: float32 [16, 128], P('ch'), may hold values from -0.5 to 0.5
- cotangent: bfloat16 [16384, 256], P(('dp', 'ctx'), 'ch'), parts along dimension 0, may hold values from -6 to 6
Outputs:
- mixed_out: bfloat16 [16384, 256], P(('dp', 'ctx'), 'ch'), parts along dimension 0
- grad_streams: bfloat16 [16384, 3, 256], P(('dp', 'ctx'), None, 'ch'), parts along dimension 0
- grad_residue: float32 [32, 16], P(('dp', 'ch')), parts along dimension 0
The draws below stay inside these ranges and needn't reach their ends.
There are 2 independent parts, one for each index of `dp`. The reference program is written for one: setup_inputs(seed, part) draws one part's arguments, and reference() takes and returns one part's arrays. A program takes and returns all parts, laid end to end along the dimension named above; an argument that names none is the same for every part. Nothing has to cross between parts.
All inputs are finite; a program needn't handle non-finite values.
Results may differ from the reference program's by a relative error of at most 0.002.
Values may be sent and summed in bfloat16 or wider, within the bound.
A program may use at most 64 MiB of HBM per device.

```python
import math
import jax
import jax.numpy as jnp
from jax import lax

M = 16
TAPS = 128
SHORT = 7
BLOCK = 128
C = 256
GROUPS = 16
L = 8192


def block_levels(own_key, dims, split, least, high):
    def one(position, parts):
        draws = jax.random.uniform(jax.random.fold_in(jax.random.fold_in(own_key, 6), position), (parts,), jnp.float32, least / len(split), high / len(split))
        return jnp.repeat(jnp.exp(draws), dims[position] // parts).reshape((-1,) + (1,) * (len(dims) - position - 1))

    level = one(*split[0])
    for cut in split[1:]:
        level = level * one(*cut)
    return level


def scatter_about(own_key, dims, scale, bound, shards=(), kind=jnp.bfloat16):
    array = scale * jax.random.normal(own_key, dims, jnp.float32)
    if shards:
        array = array * block_levels(own_key, dims, shards, -0.22, 0.18)
    return jnp.clip(array, -bound, bound).astype(kind)


def setup_inputs(seed: int = 0, part: int = 0) -> dict:
    key_of = jax.random.split(jax.random.key(seed), 7)
    part_splits = jax.random.split(jax.random.fold_in(key_of[6], part), 7)
    raw_streams = scatter_about(part_splits[0], (L, 3, C), 1.0, 6.0, ((0, 8), (2, 2)))
    short_taps = scatter_about(key_of[1], (SHORT, 3, C), 0.4, 2.4, ((2, 2),), jnp.float32)
    decay_rate = jnp.clip(jnp.exp(math.log(0.08) - 11.090355 * jax.random.uniform(key_of[2], (GROUPS, M), jnp.float32) ** block_levels(key_of[2], (GROUPS, M), ((0, 2),), -0.2, 0.2)), 1.220703097715159e-06, 0.08)
    residue = scatter_about(key_of[3], (GROUPS, M), 0.35, 2.0, ((0, 2),), jnp.float32)
    medium_filter = scatter_about(key_of[4], (GROUPS, TAPS), TAPS ** -0.5, 0.5, ((0, 2),), jnp.float32)
    cotangent = scatter_about(part_splits[5], (L, C), 1.0, 6.0, ((0, 8), (1, 2)))
    return dict(raw_streams=raw_streams, short_taps=short_taps, decay_rate=decay_rate, residue=residue, medium_filter=medium_filter, cotangent=cotangent)


def einsum_high(form, *operands):
    return jnp.einsum(form, *operands, precision=lax.Precision.HIGHEST)

def mode_stack(rate, block):
    positions = jnp.arange(block, dtype=jnp.int32)
    lagged = positions[:, None] - positions[None, :]
    lag_float = jnp.maximum(lagged, 0).astype(jnp.float32)
    return jnp.where(lagged[None, None] >= 0, jnp.exp(-rate[:, :, None, None] * lag_float[None, None]), 0.0)

def toeplitz_band(vector, block):
    groups, taps = vector.shape
    width = block + taps - 1
    padded = jnp.concatenate([vector, jnp.zeros((groups, width + 1 - taps), jnp.float32)], axis=1)
    tiled = jnp.tile(padded, (1, block))[:, :block * width]
    return tiled.reshape(groups, block, width)

def make_tables(rate, residue, medium, block):
    taps = medium.shape[1]
    scaled = jnp.sqrt(-jnp.expm1(-2.0 * rate))
    rhat = residue * scaled
    positions = jnp.arange(block, dtype=jnp.int32).astype(jnp.float32)
    after = jnp.exp(-rate[:, None, :] * (positions[None, :, None] + 1.0))
    into = jnp.exp(-rate[:, :, None] * (block - 1.0 - positions)[None, None, :])
    from_start = jnp.exp(-rate[:, :, None] * positions[None, None, :])
    to_end = rhat[:, None, :] * jnp.exp(-rate[:, None, :] * (block - positions)[None, :, None])
    whole = jnp.exp(-rate * float(block))
    stacked = mode_stack(rate, block)
    kernel = einsum_high('gm,gmts->gts', rhat, stacked)
    fwd_band = toeplitz_band(medium[:, ::-1], block)
    bwd_band = toeplitz_band(medium, block)
    fwd_prev = fwd_band[:, :, :taps - 1]
    fwd_join = kernel + fwd_band[:, :, taps - 1:]
    bwd_join = jnp.swapaxes(kernel, 1, 2) + bwd_band[:, :, :block]
    bwd_next = bwd_band[:, :, block:]
    return (rhat, after, into, from_start, to_end, whole, fwd_join, fwd_prev, bwd_join, bwd_next, stacked)

def forward_blocks(product, head, state_init, tables, block):
    rhat, after, into, from_start, to_end, whole, fwd_join, fwd_prev, bwd_join, bwd_next, stacked = tables
    lifted = rhat[:, None, :] * after
    rim = head.shape[0]
    count = product.shape[0] // block
    pieces = product.reshape((count, block) + product.shape[1:])
    prevs = jnp.concatenate([head[None], pieces[:-1, block - rim:]], axis=0)

    def step(state, pair):
        piece, prev = pair
        mixed = einsum_high('gts,sgc->tgc', fwd_join, piece) + einsum_high('gtm,gcm->tgc', lifted, state)
        mixed = mixed + einsum_high('gts,sgc->tgc', fwd_prev, prev)
        renewed = whole[:, None, :] * state + einsum_high('gms,sgc->gcm', into, piece)
        return (renewed, (mixed, state))
    _, (outputs, starts) = lax.scan(step, state_init, (pieces, prevs))
    return (outputs.reshape(product.shape), starts)

def backward_blocks(grad_mixed, grad_tail, product, starts, carry_init, tables, block, rate):
    rhat, after, into, from_start, to_end, whole, fwd_join, fwd_prev, bwd_join, bwd_next, stacked = tables
    rim = grad_tail.shape[0]
    count = product.shape[0] // block
    grad_pieces = grad_mixed.reshape((count, block) + grad_mixed.shape[1:])
    pieces = product.reshape((count, block) + product.shape[1:])
    nexts = jnp.concatenate([grad_pieces[1:, :rim], grad_tail[None]], axis=0)

    def step(carry, items):
        grad_state, running = carry
        grad_piece, following, piece, state = items
        grad_prod = einsum_high('gst,tgc->sgc', bwd_join, grad_piece) + einsum_high('gsm,gcm->sgc', to_end, grad_state)
        grad_prod = grad_prod + einsum_high('gst,tgc->sgc', bwd_next, following)
        renewed = whole[:, None, :] * grad_state + einsum_high('gmt,tgc->gcm', from_start, grad_piece)
        cross = einsum_high('tgc,sgc->gts', grad_piece, piece)
        inner = einsum_high('gts,gmts->gm', cross, stacked)
        running = running + inner + einsum_high('gtm,gcm,tgc->gm', after, state, grad_piece)
        return ((renewed, running), grad_prod)
    zero_total = jnp.zeros(rate.shape, jnp.float32)
    (_, running), grads = lax.scan(step, (carry_init, zero_total), (grad_pieces, nexts, pieces, starts), reverse=True)
    return (grads.reshape(product.shape), running)

def short_filter(extended, weights, rows):
    short = weights.shape[0]
    total = weights[0] * extended[short - 1:short - 1 + rows]
    for shift_by in range(1, short):
        total = total + weights[shift_by] * extended[short - 1 - shift_by:short - 1 - shift_by + rows]
    return total

def short_adjoint(extended, weights, rows):
    total = weights[0] * extended[0:rows]
    for shift_by in range(1, weights.shape[0]):
        total = total + weights[shift_by] * extended[shift_by:shift_by + rows]
    return total

def reference(raw_streams, short_taps, decay_rate, residue, medium_filter, cotangent):
    length = raw_streams.shape[0]
    chans = raw_streams.shape[2]
    groups, modes = decay_rate.shape
    per_group = chans // groups
    short = short_taps.shape[0]
    taps = medium_filter.shape[1]
    extended = jnp.concatenate([jnp.zeros((short - 1, 3, chans), jnp.float32), raw_streams.astype(jnp.float32)])
    featured = short_filter(extended, short_taps, length)
    query = featured[:, 0]
    keys = featured[:, 1]
    values = featured[:, 2]
    product = (keys * values).reshape(length, groups, per_group)
    head = jnp.zeros((taps - 1, groups, per_group), jnp.float32)
    tables = make_tables(decay_rate, residue, medium_filter, BLOCK)
    zero_state = jnp.zeros((groups, per_group, modes), jnp.float32)
    mixed, starts = forward_blocks(product, head, zero_state, tables, BLOCK)
    mixed = mixed.reshape(length, chans)
    mixed_out = (query * mixed).astype(jnp.bfloat16)
    grad_out = cotangent.astype(jnp.float32)
    grad_mixed = (grad_out * query).reshape(length, groups, per_group)
    grad_query = grad_out * mixed
    tail = jnp.zeros((taps - 1, groups, per_group), jnp.float32)
    grad_prod, running = backward_blocks(grad_mixed, tail, product, starts, zero_state, tables, BLOCK, decay_rate)
    grad_prod = grad_prod.reshape(length, chans)
    grad_featured = jnp.stack([grad_query, grad_prod * values, grad_prod * keys], axis=1)
    grad_padded = jnp.concatenate([grad_featured, jnp.zeros((short - 1, 3, chans), jnp.float32)])
    grad_streams = short_adjoint(grad_padded, short_taps, length).astype(jnp.bfloat16)
    scaled = jnp.sqrt(-jnp.expm1(-2.0 * decay_rate))
    grad_residue = running * scaled / math.sqrt(float(length * per_group))
    return (mixed_out, grad_streams, grad_residue)
```

```python
import functools
import math

import jax
import jax.numpy as jnp
from jax import lax
from jax.experimental import pallas as pl
from jax.experimental.pallas import tpu as pltpu
from jax.sharding import PartitionSpec as P

F32 = jnp.float32
BF16 = jnp.bfloat16
MESH = pl.DeviceIdType.MESH
B = 128
HIGH = lax.Precision.HIGHEST


def dot(a, b, ca, cb):
    return lax.dot_general(
        a, b, (((ca,), (cb,)), ((), ())), precision=HIGH, preferred_element_type=F32
    )


def lanes(shape):
    return lax.broadcasted_iota(jnp.int32, shape, 1)


def rolled(x, shift):
    shift = shift % x.shape[1]
    return pltpu.roll(x, shift, 1) if shift else x


def block_transpose(xs, width):
    count = len(xs)
    chunk = lanes(xs[0].shape) // width
    xs = list(xs)
    bit = 1
    while bit < count:
        high = (chunk & bit) != 0
        for i in range(count):
            if i & bit == 0:
                a, d = xs[i], xs[i | bit]
                xs[i] = jnp.where(high, rolled(d, width * bit), a)
                xs[i | bit] = jnp.where(high, d, rolled(a, -width * bit))
        bit *= 2
    return xs


def kernel(
    n, groups, modes,
    raw, taps, cot, rate_ref, rhat_ref, ratec_ref, w_ref,
    mixed_out, grad_out, res_out,
    hkv, hq, nq, ncot, ext, feat, hext, qext, yp, yg, head, tail,
    s_all, u_all, msg1, msg2, got1, got2, of, ob, gf, gfr,
    hs, hr, m1s, m1r, m2s, m2r, gs, gr,
):
    rows, chans = cot.shape
    per = chans // groups
    count = rows // B
    short = taps.shape[1]
    me = lax.axis_index("ctx")
    nxt = lax.rem(me + 1, n)
    prv = lax.rem(me + n - 1, n)
    barrier = pltpu.get_barrier_semaphore()
    for k in range(1, n):
        pl.semaphore_signal(
            barrier, inc=1, device_id={"ctx": lax.rem(me + k, n)}, device_id_type=MESH
        )
    pl.semaphore_wait(barrier, n - 1)

    def send(src, dst, ssem, rsem, to):
        copy = pltpu.make_async_remote_copy(
            src_ref=src, dst_ref=dst, send_sem=ssem, recv_sem=rsem,
            device_id={"ctx": to}, device_id_type=MESH,
        )
        copy.start()
        return copy

    halo = [
        send(raw.at[0:1, rows - 16 : rows], hq, hs.at[0], hr.at[0], nxt),
        send(raw.at[1:3, rows - 144 : rows], hkv, hs.at[1], hr.at[1], nxt),
        send(raw.at[0:1, 0:B], nq, hs.at[2], hr.at[2], prv),
        send(cot.at[0:B], ncot, hs.at[3], hr.at[3], prv),
    ]

    has_prev = jnp.where(me > 0, 1.0, 0.0).astype(F32)
    has_next = jnp.where(me < n - 1, 1.0, 0.0).astype(F32)
    tap = [[taps[i, k : k + 1, :] for k in range(short)] for i in range(3)]

    def filtered(ref, i, slot, start, size):
        total = tap[i][0] * ref[slot, start : start + size, :]
        for k in range(1, short):
            total = total + tap[i][k] * ref[slot, start - k : start - k + size, :]
        return total

    for j in range(count):
        for i in range(3):
            ext[i, 8 + j * B : 8 + (j + 1) * B, :] = raw[i, j * B : (j + 1) * B, :].astype(F32)
    rate = rate_ref[...]
    rhat = rhat_ref[...]
    lane = lanes(rate.shape)
    lane_f = lane.astype(F32)
    e0 = jnp.exp(-rate * lane_f)
    e3 = jnp.exp(-rate * (B - 1.0 - lane_f))
    lam = jnp.exp(-rate)

    for copy in halo:
        copy.wait()
    ext[0, 0:8, :] = hq[0].astype(F32)[8:16] * has_prev
    for i in (1, 2):
        full = hkv[i - 1].astype(F32) * has_prev
        hext[i - 1] = full
        ext[i, 0:8, :] = full[136:144]
    qext[0, 0:8, :] = ext[0, rows : rows + 8, :]
    qext[0, 8 : 8 + B, :] = nq[0].astype(F32)
    for j in range(count):
        for i in range(3):
            feat[i, j * B : (j + 1) * B, :] = filtered(ext, i, i, 8 + j * B, B)
    head[...] = filtered(hext, 1, 0, 16, B) * filtered(hext, 2, 1, 16, B)
    tail[...] = filtered(qext, 0, 0, 8, B) * ncot[...].astype(F32) * has_next

    sub = 16

    def to_groups(t, _):
        products, grads = [], []
        for j in range(count):
            here = pl.ds(pl.multiple_of(j * B + t * sub, sub), sub)
            products.append(feat[1, here, :] * feat[2, here, :])
            grads.append(cot[here, :].astype(F32) * feat[0, here, :])
        there = pl.ds(pl.multiple_of(t * sub, sub), sub)
        for g, y in enumerate(block_transpose(products, per)):
            yp[g, there, :] = y
        for g, y in enumerate(block_transpose(grads, per)):
            yg[g, there, :] = y
        return 0

    lax.fori_loop(0, B // sub, to_groups, 0)

    for g in range(groups):
        at = slice(g * modes, (g + 1) * modes)
        s_all[at, :] = dot(e3[at], yp[g], 1, 0)
        u_all[at, :] = dot(e0[at], yg[g], 1, 0)

    state = s_all[...]
    adj = u_all[...]
    u = adj
    step = 1
    while step < count:
        decay = jnp.exp(-rate * float(B * step))
        width = per * step
        state = state + decay * jnp.where(lane >= width, rolled(state, width), 0.0)
        adj = adj + decay * jnp.where(lane < chans - width, rolled(adj, -width), 0.0)
        step *= 2
    starts = jnp.where(lane >= per, rolled(state, per), 0.0)
    ends = jnp.where(lane < chans - per, rolled(adj, -per), 0.0)

    small = lanes((modes, chans)) // per
    final = jnp.zeros((modes, chans), F32)
    first = jnp.zeros((modes, chans), F32)
    for g in range(groups):
        at = slice(g * modes, (g + 1) * modes)
        final = jnp.where(small == g, rolled(state[at], g * per - (count - 1) * per), final)
        first = jnp.where(small == g, rolled(adj[at], g * per), first)
    msg1[0:modes, :] = final
    msg1[modes : 2 * modes, :] = first
    got1[me] = msg1[...]
    sent = []
    for k in range(1, n):
        sent.append(send(msg1, got1.at[me], m1s.at[k], m1r.at[me], lax.rem(me + k, n)))

    up = jnp.exp(rate * lane_f)
    local = lam * starts * u
    terms = jnp.zeros((modes, chans), F32)
    square_l = lanes((B, B))
    square_s = lax.broadcasted_iota(jnp.int32, (B, B), 0)
    for g in range(groups):
        at = slice(g * modes, (g + 1) * modes)
        cross = dot(yg[g], yp[g], 1, 1)
        cross = jnp.where(square_s >= square_l, cross, 0.0)
        inner = dot(up[at], cross, 1, 1) * e0[at] + local[at]
        terms = jnp.where(small == g, jnp.sum(inner, axis=1, keepdims=True), terms)
    msg2[...] = terms
    got2[me] = terms
    for k in range(1, n):
        sent.append(send(msg2, got2.at[me], m2s.at[k], m2r.at[me], lax.rem(me + k, n)))

    wide = lanes((B, 2 * B))
    for g in range(groups):
        def band(which):
            row = jnp.broadcast_to(w_ref[which, g : g + 1, :], (B, 2 * B))
            return pltpu.roll(row, 0, 1, stride=1, stride_axis=0)

        fwd = band(0) + jnp.where(wide >= B, band(1), 0.0)
        bwd = band(2) + jnp.where(wide < B, band(3), 0.0)
        cur = yp[g]
        prev = jnp.where(square_l >= per, rolled(cur, per), rolled(head[...], -g * per))
        of[g] = dot(fwd[:, :B], prev, 1, 0) + dot(fwd[:, B:], cur, 1, 0)
        cur = yg[g]
        after = jnp.where(
            square_l < chans - per, rolled(cur, -per), rolled(tail[...], chans - per - g * per)
        )
        ob[g] = dot(bwd[:, :B], cur, 1, 0) + dot(bwd[:, B:], after, 1, 0)

    for k in range(1, n):
        peer = lax.rem(me + k, n)
        pltpu.make_async_remote_copy(
            src_ref=msg1, dst_ref=got1.at[peer], send_sem=m1s.at[k], recv_sem=m1r.at[peer],
            device_id={"ctx": peer}, device_id_type=MESH,
        ).wait_recv()

    whole = jnp.exp(-ratec_ref[...] * float(rows))
    lamc = jnp.exp(-ratec_ref[...])
    zero = jnp.zeros((modes, chans), F32)
    run, carry, crossed = zero, zero, zero
    for d in range(n):
        block = got1[d]
        carry = jnp.where(me == d, run, carry)
        crossed = crossed + run * block[modes:]
        run = whole * run + block[:modes]
    run, back = zero, zero
    for d in reversed(range(n)):
        back = jnp.where(me == d, run, back)
        run = whole * run + got1[d][modes:]
    crossed = crossed * lamc

    def spread(x):
        pieces = []
        for g in range(groups):
            pieces.append(jnp.where(small == 0, rolled(x, -g * per), 0.0))
        y = jnp.concatenate(pieces, axis=0)
        width = per
        while width < chans:
            y = y + rolled(y, width)
            width *= 2
        return y

    block_f = (lane // per).astype(F32)
    starts = rhat * (starts + jnp.exp(-rate * (B * block_f)) * spread(carry))
    ends = rhat * (ends + jnp.exp(-rate * (B * (count - 1.0 - block_f))) * spread(back))
    e1 = e0 * lam
    e2 = e3 * lam
    for g in range(groups):
        at = slice(g * modes, (g + 1) * modes)
        of[g] = of[g] + dot(e1[at], starts[at], 0, 0)
        ob[g] = ob[g] + dot(e2[at], ends[at], 0, 0)

    def from_groups(t, _):
        there = pl.ds(pl.multiple_of(t * sub, sub), sub)
        mixed = block_transpose([of[g, there, :] for g in range(groups)], per)
        grads = block_transpose([ob[g, there, :] for g in range(groups)], per)
        for j in range(count):
            here = pl.ds(pl.multiple_of(j * B + t * sub, sub), sub)
            mixed_out[here, :] = (feat[0, here, :] * mixed[j]).astype(BF16)
            gf[0, here, :] = cot[here, :].astype(F32) * mixed[j]
            gf[1, here, :] = grads[j] * feat[2, here, :]
            gf[2, here, :] = grads[j] * feat[1, here, :]
        return 0

    lax.fori_loop(0, B // sub, from_groups, 0)
    last = send(gf.at[:, 0:8], gfr, gs, gr, prv)

    def adjoint(i, start, size):
        total = tap[i][0] * gf[i, start : start + size, :]
        for k in range(1, short):
            total = total + tap[i][k] * gf[i, start + k : start + k + size, :]
        return total

    for j in range(count - 1):
        for i in range(3):
            grad_out[i, j * B : (j + 1) * B, :] = adjoint(i, j * B, B).astype(BF16)
    for k in range(1, n):
        peer = lax.rem(me + k, n)
        pltpu.make_async_remote_copy(
            src_ref=msg2, dst_ref=got2.at[peer], send_sem=m2s.at[k], recv_sem=m2r.at[peer],
            device_id={"ctx": peer}, device_id_type=MESH,
        ).wait_recv()
    total = got2[0]
    for d in range(1, n):
        total = total + got2[d]
    summed = zero
    for g in range(groups):
        part = jnp.sum(jnp.where(small == g, crossed, 0.0), axis=1, keepdims=True)
        summed = jnp.where(small == g, part, summed)
    res_out[...] = total + summed
    last.wait()
    gf[:, rows : rows + 8, :] = gfr[...] * has_next
    for i in range(3):
        grad_out[i, rows - B : rows, :] = adjoint(i, rows - B, B).astype(BF16)
    for copy in sent:
        copy.wait_send()


def body(n, raw_streams, short_taps, decay_rate, residue, medium_filter, cotangent):
    rows, _, chans = raw_streams.shape
    groups, modes = decay_rate.shape
    per = chans // groups
    raw = jnp.transpose(raw_streams, (1, 0, 2))
    taps = jnp.transpose(short_taps, (1, 0, 2))
    scaled = jnp.sqrt(-jnp.expm1(-2.0 * decay_rate))
    rhat = residue * scaled
    lag = jnp.arange(B, dtype=jnp.int32).astype(F32)
    h = jnp.sum(rhat[:, :, None] * jnp.exp(-decay_rate[:, :, None] * lag), axis=1)

    def reverse(v):
        return jnp.pad(v[:, ::-1], ((0, 0), (1, B - 1)))

    def plain(v):
        return jnp.pad(v, ((0, 0), (0, B)))

    w = jnp.stack([reverse(medium_filter), reverse(h), plain(medium_filter), plain(h)])
    rate_rows = jnp.broadcast_to(decay_rate.reshape(groups * modes, 1), (groups * modes, B))
    rhat_rows = jnp.broadcast_to(rhat.reshape(groups * modes, 1), (groups * modes, B))
    rate_cols = jnp.repeat(decay_rate.T, per, axis=1)
    vm = pltpu.VMEM
    dma = pltpu.SemaphoreType.DMA
    spec = pl.BlockSpec(memory_space=pltpu.VMEM)
    mixed, grads, res = pl.pallas_call(
        functools.partial(kernel, n, groups, modes),
        out_shape=(
            jax.ShapeDtypeStruct((rows, chans), BF16),
            jax.ShapeDtypeStruct((3, rows, chans), BF16),
            jax.ShapeDtypeStruct((modes, chans), F32),
        ),
        in_specs=[spec] * 7,
        out_specs=(spec, spec, spec),
        scratch_shapes=[
            vm((2, 144, chans), BF16), vm((1, 16, chans), BF16),
            vm((1, B, chans), BF16), vm((B, chans), BF16),
            vm((3, rows + 8, chans), F32), vm((3, rows, chans), F32),
            vm((2, 144, chans), F32), vm((1, B + 8, chans), F32),
            vm((groups, B, chans), F32), vm((groups, B, chans), F32),
            vm((B, chans), F32), vm((B, chans), F32),
            vm((groups * modes, chans), F32), vm((groups * modes, chans), F32),
            vm((2 * modes, chans), F32), vm((modes, chans), F32),
            vm((n, 2 * modes, chans), F32), vm((n, modes, chans), F32),
            vm((groups, B, chans), F32), vm((groups, B, chans), F32),
            vm((3, rows + 8, chans), F32), vm((3, 8, chans), F32),
            dma((4,)), dma((4,)), dma((n,)), dma((n,)), dma((n,)), dma((n,)), dma, dma,
        ],
        compiler_params=pltpu.CompilerParams(
            collective_id=0, has_side_effects=True, vmem_limit_bytes=48 * 2**20
        ),
    )(raw, taps, cotangent, rate_rows, rhat_rows, rate_cols, w)
    grad_residue = res[:, ::per].T * scaled / math.sqrt(float(rows * n * per))
    return mixed, jnp.transpose(grads, (1, 0, 2)), grad_residue


def solution(mesh):
    in_specs = (
        P(("dp", "ctx"), None, "ch"),
        P(None, None, "ch"),
        P("ch", None),
        P("ch", None),
        P("ch", None),
        P(("dp", "ctx"), "ch"),
    )
    out_specs = (P(("dp", "ctx"), "ch"), P(("dp", "ctx"), None, "ch"), P(("dp", "ch"), None))
    return jax.shard_map(
        functools.partial(body, mesh.shape["ctx"]),
        mesh=mesh, in_specs=in_specs, out_specs=out_specs, check_vma=False,
    )
```

```python
import functools
import math

import jax
import jax.numpy as jnp
from jax import lax
from jax.experimental import pallas as pl
from jax.experimental.pallas import tpu as pltpu
from jax.sharding import PartitionSpec as P

F32 = jnp.float32
BF16 = jnp.bfloat16
MESH = pl.DeviceIdType.MESH
B = 128


def halves(x):
    hi = x.astype(BF16)
    return hi, (x - hi.astype(F32)).astype(BF16)


def quadrants(a, b, cb):
    out = lax.dot_general(a, b, (((1,), (cb,)), ((), ())), preferred_element_type=F32)
    r, c = out.shape[0] // 2, out.shape[1] // 2
    return (out[:r, :c] + out[:r, c:]) + (out[r:, :c] + out[r:, c:])


def tall(x):
    return jnp.concatenate(halves(x), axis=0)


def flat(x):
    return jnp.concatenate(halves(x), axis=1)


def lanes(shape):
    return lax.broadcasted_iota(jnp.int32, shape, 1)


def rolled(x, shift):
    shift = shift % x.shape[1]
    return pltpu.roll(x, shift, 1) if shift else x


def block_transpose(xs, width):
    count = len(xs)
    chunk = lanes(xs[0].shape) // width
    xs = list(xs)
    bit = 1
    while bit < count:
        high = (chunk & bit) != 0
        for i in range(count):
            if i & bit == 0:
                a, d = xs[i], xs[i | bit]
                xs[i] = jnp.where(high, rolled(d, width * bit), a)
                xs[i | bit] = jnp.where(high, d, rolled(a, -width * bit))
        bit *= 2
    return xs


def kernel(
    n, groups, modes,
    raw_hbm, taps, cot_hbm, rate_ref, rhat_ref, rev_ref, med_ref,
    mixed_out, grad_out, res_out,
    raw, cot, tf, tb, ls,
    hkv, hq, nq, ncot, ext, feat, hext, qext, yp, yg, head, tail,
    s_all, u_all, msg1, msg2, got1, got2, of, ob, gf, gfr,
    hs, hr, m1s, m1r, m2s, m2r, gs, gr,
):
    rows, chans = cot.shape
    per = chans // groups
    count = rows // B
    short = taps.shape[1]
    loads = [pltpu.make_async_copy(raw_hbm.at[i], raw.at[i], ls.at[i]) for i in range(3)]
    loads.append(pltpu.make_async_copy(cot_hbm, cot, ls.at[3]))
    for i in (1, 2, 0, 3):
        loads[i].start()
    me = lax.axis_index("ctx")
    nxt = lax.rem(me + 1, n)
    prv = lax.rem(me + n - 1, n)
    barrier = pltpu.get_barrier_semaphore()
    for k in range(1, n):
        pl.semaphore_signal(
            barrier, inc=1, device_id={"ctx": lax.rem(me + k, n)}, device_id_type=MESH
        )
    pl.semaphore_wait(barrier, n - 1)

    def send(src, dst, ssem, rsem, to):
        copy = pltpu.make_async_remote_copy(
            src_ref=src, dst_ref=dst, send_sem=ssem, recv_sem=rsem,
            device_id={"ctx": to}, device_id_type=MESH,
        )
        copy.start()
        return copy

    halo = [
        send(raw_hbm.at[0:1, rows - 16 : rows], hq, hs.at[0], hr.at[0], nxt),
        send(raw_hbm.at[1:3, rows - 144 : rows], hkv, hs.at[1], hr.at[1], nxt),
        send(raw_hbm.at[0:1, 0:B], nq, hs.at[2], hr.at[2], prv),
        send(cot_hbm.at[0:B], ncot, hs.at[3], hr.at[3], prv),
    ]

    has_prev = jnp.where(me > 0, 1.0, 0.0).astype(F32)
    has_next = jnp.where(me < n - 1, 1.0, 0.0).astype(F32)
    tap = [[taps[i, k : k + 1, :] for k in range(short)] for i in range(3)]

    def filtered(ref, i, slot, start, size):
        total = tap[i][0] * ref[slot, start : start + size, :]
        for k in range(1, short):
            total = total + tap[i][k] * ref[slot, start - k : start - k + size, :]
        return total

    def expanded(ref):
        tile = jnp.concatenate(
            [jnp.broadcast_to(ref[g : g + 1, :], (modes, modes)) for g in range(groups)], axis=0
        )
        row = lax.broadcasted_iota(jnp.int32, tile.shape, 0) % modes
        column = jnp.sum(jnp.where(lanes(tile.shape) == row, tile, 0.0), axis=1, keepdims=True)
        return jnp.broadcast_to(column, (groups * modes, B))

    rate = expanded(rate_ref)
    rhat = expanded(rhat_ref)
    lane = lanes(rate.shape)
    lane_f = lane.astype(F32)
    e0 = jnp.exp(-rate * lane_f)
    e2 = jnp.exp(-rate * (B - lane_f))
    e3 = jnp.exp(-rate * (B - 1.0 - lane_f))
    lam = jnp.exp(-rate)
    sub_i = lax.broadcasted_iota(jnp.int32, rate.shape, 0)
    sub_f = sub_i.astype(F32)
    rate_row = jnp.sum(jnp.where(sub_i == lane, rate, 0.0), axis=0, keepdims=True)
    e1t = flat(jnp.exp(-rate_row * (sub_f + 1.0)))
    e2t = flat(jnp.exp(-rate_row * (B - sub_f)))
    square_l, square_s = lane, sub_i

    wide = lanes((B, 2 * B))
    for g in range(groups):
        at = slice(g * modes, (g + 1) * modes)
        hb = jnp.sum(rhat[at] * e0[at], axis=0, keepdims=True)
        hf = jnp.sum(rhat[at] * e2[at], axis=0, keepdims=True)
        row_l = lanes(hb.shape)
        zrow = jnp.zeros_like(hb)
        hf = jnp.where(row_l == 0, 0.0, hf)
        first_h = jnp.where(row_l == 0, hb, 0.0)

        def band(row):
            row = jnp.broadcast_to(row, (B, 2 * B))
            return pltpu.roll(row, 0, 1, stride=1, stride_axis=0)

        fwd_h = band(jnp.concatenate([hf, first_h], axis=1))
        bwd_h = band(jnp.concatenate([hb, zrow], axis=1))
        bwd_m = band(jnp.concatenate([med_ref[g : g + 1, :], zrow], axis=1))
        tf[g] = tall(band(rev_ref[g : g + 1, :]) + jnp.where(wide >= B, fwd_h, 0.0))
        tb[g] = tall(bwd_m + jnp.where(wide < B, bwd_h, 0.0))

    for i in (1, 2, 0):
        loads[i].wait()
        for j in range(count):
            ext[i, 8 + j * B : 8 + (j + 1) * B, :] = raw[i, j * B : (j + 1) * B, :].astype(F32)
        for j in range(1, count):
            feat[i, j * B : (j + 1) * B, :] = filtered(ext, i, i, 8 + j * B, B)
    loads[3].wait()

    for copy in halo:
        copy.wait()
    ext[0, 0:8, :] = hq[0].astype(F32)[8:16] * has_prev
    for i in (1, 2):
        full = hkv[i - 1].astype(F32) * has_prev
        hext[i - 1] = full
        ext[i, 0:8, :] = full[136:144]
    qext[0, 0:8, :] = ext[0, rows : rows + 8, :]
    qext[0, 8 : 8 + B, :] = nq[0].astype(F32)
    for i in range(3):
        feat[i, 0:B, :] = filtered(ext, i, i, 8, B)
    head[...] = filtered(hext, 1, 0, 16, B) * filtered(hext, 2, 1, 16, B)
    tail[...] = filtered(qext, 0, 0, 8, B) * ncot[...].astype(F32) * has_next

    sub = 16

    def to_groups(t, _):
        products, grads = [], []
        for j in range(count):
            here = pl.ds(pl.multiple_of(j * B + t * sub, sub), sub)
            products.append(feat[1, here, :] * feat[2, here, :])
            grads.append(cot[here, :].astype(F32) * feat[0, here, :])
        there = pl.ds(pl.multiple_of(t * sub, sub), sub)
        for g, y in enumerate(block_transpose(products, per)):
            yp[g, there, :] = y
        for g, y in enumerate(block_transpose(grads, per)):
            yg[g, there, :] = y
        return 0

    lax.fori_loop(0, B // sub, to_groups, 0, unroll=B // sub)

    for g in range(groups):
        at = slice(g * modes, (g + 1) * modes)
        s_all[at, :] = quadrants(tall(e3[at]), flat(yp[g]), 0)
        u_all[at, :] = quadrants(tall(e0[at]), flat(yg[g]), 0)

    state = s_all[...]
    adj = u_all[...]
    u = adj
    step = 1
    while step < count:
        decay = jnp.exp(-rate * float(B * step))
        width = per * step
        state = state + decay * jnp.where(lane >= width, rolled(state, width), 0.0)
        adj = adj + decay * jnp.where(lane < chans - width, rolled(adj, -width), 0.0)
        step *= 2
    starts = jnp.where(lane >= per, rolled(state, per), 0.0)
    ends = jnp.where(lane < chans - per, rolled(adj, -per), 0.0)

    small = lanes((modes, chans)) // per
    final = jnp.zeros((modes, chans), F32)
    first = jnp.zeros((modes, chans), F32)
    for g in range(groups):
        at = slice(g * modes, (g + 1) * modes)
        final = jnp.where(small == g, rolled(state[at], g * per - (count - 1) * per), final)
        first = jnp.where(small == g, rolled(adj[at], g * per), first)
    msg1[0:modes, :] = final
    msg1[modes : 2 * modes, :] = first
    got1[me] = msg1[...]
    sent = []
    for k in range(1, n):
        sent.append(send(msg1, got1.at[me], m1s.at[k], m1r.at[me], lax.rem(me + k, n)))

    up = jnp.exp(rate * lane_f)
    local = lam * starts * u
    terms = jnp.zeros((modes, chans), F32)
    for g in range(groups):
        at = slice(g * modes, (g + 1) * modes)
        cross = quadrants(tall(yg[g]), tall(yp[g]), 1)
        cross = jnp.where(square_s >= square_l, cross, 0.0)
        inner = quadrants(tall(up[at]), tall(cross), 1) * e0[at] + local[at]
        terms = jnp.where(small == g, jnp.sum(inner, axis=1, keepdims=True), terms)
    msg2[...] = terms
    got2[me] = terms
    for k in range(1, n):
        sent.append(send(msg2, got2.at[me], m2s.at[k], m2r.at[me], lax.rem(me + k, n)))

    for g in range(groups):
        cur = yp[g]
        prev = jnp.where(square_l >= per, rolled(cur, per), rolled(head[...], -g * per))
        of[g] = quadrants(tf[g], jnp.concatenate([flat(prev), flat(cur)], axis=0), 0)
        cur = yg[g]
        after = jnp.where(
            square_l < chans - per, rolled(cur, -per), rolled(tail[...], chans - per - g * per)
        )
        ob[g] = quadrants(tb[g], jnp.concatenate([flat(cur), flat(after)], axis=0), 0)

    for k in range(1, n):
        peer = lax.rem(me + k, n)
        pltpu.make_async_remote_copy(
            src_ref=msg1, dst_ref=got1.at[peer], send_sem=m1s.at[k], recv_sem=m1r.at[peer],
            device_id={"ctx": peer}, device_id_type=MESH,
        ).wait_recv()

    rate_c = jnp.zeros((modes, chans), F32)
    for g in range(groups):
        rate_c = jnp.where(small == g, rate[g * modes : (g + 1) * modes], rate_c)
    whole = jnp.exp(-rate_c * float(rows))
    lamc = jnp.exp(-rate_c)
    zero = jnp.zeros((modes, chans), F32)
    run, carry, crossed = zero, zero, zero
    for d in range(n):
        block = got1[d]
        carry = jnp.where(me == d, run, carry)
        crossed = crossed + run * block[modes:]
        run = whole * run + block[:modes]
    run, back = zero, zero
    for d in reversed(range(n)):
        back = jnp.where(me == d, run, back)
        run = whole * run + got1[d][modes:]
    crossed = crossed * lamc

    def spread(x):
        pieces = []
        for g in range(groups):
            pieces.append(jnp.where(small == 0, rolled(x, -g * per), 0.0))
        y = jnp.concatenate(pieces, axis=0)
        width = per
        while width < chans:
            y = y + rolled(y, width)
            width *= 2
        return y

    block_f = (lane // per).astype(F32)
    starts = rhat * (starts + jnp.exp(-rate * (B * block_f)) * spread(carry))
    ends = rhat * (ends + jnp.exp(-rate * (B * (count - 1.0 - block_f))) * spread(back))
    starts = flat(starts)
    ends = flat(ends)

    def carried(table, state, g):
        parts = [state[g * modes : (g + 1) * modes]]
        if g:
            parts.insert(0, jnp.zeros((g * modes, 2 * chans), BF16))
        if g < groups - 1:
            parts.append(jnp.zeros(((groups - 1 - g) * modes, 2 * chans), BF16))
        z = jnp.concatenate(parts, axis=0)
        out = lax.dot_general(
            table, jnp.concatenate([z, z], axis=0), (((1,), (0,)), ((), ())),
            preferred_element_type=F32,
        )
        return out[:, :chans] + out[:, chans:]

    for g in range(groups):
        of[g] = of[g] + carried(e1t, starts, g)
        ob[g] = ob[g] + carried(e2t, ends, g)

    def from_groups(t, _):
        there = pl.ds(pl.multiple_of(t * sub, sub), sub)
        mixed = block_transpose([of[g, there, :] for g in range(groups)], per)
        grads = block_transpose([ob[g, there, :] for g in range(groups)], per)
        for j in range(count):
            here = pl.ds(pl.multiple_of(j * B + t * sub, sub), sub)
            mixed_out[here, :] = (feat[0, here, :] * mixed[j]).astype(BF16)
            gf[0, here, :] = cot[here, :].astype(F32) * mixed[j]
            gf[1, here, :] = grads[j] * feat[2, here, :]
            gf[2, here, :] = grads[j] * feat[1, here, :]
        return 0

    lax.fori_loop(0, B // sub, from_groups, 0, unroll=B // sub)
    last = send(gf.at[:, 0:8], gfr, gs, gr, prv)

    def adjoint(i, start, size):
        total = tap[i][0] * gf[i, start : start + size, :]
        for k in range(1, short):
            total = total + tap[i][k] * gf[i, start + k : start + k + size, :]
        return total

    for j in range(count - 1):
        for i in range(3):
            grad_out[i, j * B : (j + 1) * B, :] = adjoint(i, j * B, B).astype(BF16)
    for k in range(1, n):
        peer = lax.rem(me + k, n)
        pltpu.make_async_remote_copy(
            src_ref=msg2, dst_ref=got2.at[peer], send_sem=m2s.at[k], recv_sem=m2r.at[peer],
            device_id={"ctx": peer}, device_id_type=MESH,
        ).wait_recv()
    total = got2[0]
    for d in range(1, n):
        total = total + got2[d]
    summed = zero
    for g in range(groups):
        part = jnp.sum(jnp.where(small == g, crossed, 0.0), axis=1, keepdims=True)
        summed = jnp.where(small == g, part, summed)
    res_out[...] = total + summed
    last.wait()
    gf[:, rows : rows + 8, :] = gfr[...] * has_next
    for i in range(3):
        grad_out[i, rows - B : rows, :] = adjoint(i, rows - B, B).astype(BF16)
    for copy in sent:
        copy.wait_send()


def body(n, raw_streams, short_taps, decay_rate, residue, medium_filter, cotangent):
    rows, _, chans = raw_streams.shape
    groups, modes = decay_rate.shape
    per = chans // groups
    raw = jnp.transpose(raw_streams, (1, 0, 2))
    taps = jnp.transpose(short_taps, (1, 0, 2))
    scaled = jnp.sqrt(-jnp.expm1(-2.0 * decay_rate))
    rhat = residue * scaled
    rev = jnp.pad(medium_filter[:, ::-1], ((0, 0), (1, B - 1)))
    vm = pltpu.VMEM
    dma = pltpu.SemaphoreType.DMA
    hbm = pl.BlockSpec(memory_space=pltpu.HBM)
    spec = pl.BlockSpec(memory_space=pltpu.VMEM)
    mixed, grads, res = pl.pallas_call(
        functools.partial(kernel, n, groups, modes),
        out_shape=(
            jax.ShapeDtypeStruct((rows, chans), BF16),
            jax.ShapeDtypeStruct((3, rows, chans), BF16),
            jax.ShapeDtypeStruct((modes, chans), F32),
        ),
        in_specs=[hbm, spec, hbm, spec, spec, spec, spec],
        out_specs=(spec, spec, spec),
        scratch_shapes=[
            vm((3, rows, chans), BF16), vm((rows, chans), BF16),
            vm((groups, 2 * B, 2 * B), BF16), vm((groups, 2 * B, 2 * B), BF16), dma((4,)),
            vm((2, 144, chans), BF16), vm((1, 16, chans), BF16),
            vm((1, B, chans), BF16), vm((B, chans), BF16),
            vm((3, rows + 8, chans), F32), vm((3, rows, chans), F32),
            vm((2, 144, chans), F32), vm((1, B + 8, chans), F32),
            vm((groups, B, chans), F32), vm((groups, B, chans), F32),
            vm((B, chans), F32), vm((B, chans), F32),
            vm((groups * modes, chans), F32), vm((groups * modes, chans), F32),
            vm((2 * modes, chans), F32), vm((modes, chans), F32),
            vm((n, 2 * modes, chans), F32), vm((n, modes, chans), F32),
            vm((groups, B, chans), F32), vm((groups, B, chans), F32),
            vm((3, rows + 8, chans), F32), vm((3, 8, chans), F32),
            dma((4,)), dma((4,)), dma((n,)), dma((n,)), dma((n,)), dma((n,)), dma, dma,
        ],
        compiler_params=pltpu.CompilerParams(
            collective_id=0, has_side_effects=True, vmem_limit_bytes=48 * 2**20
        ),
    )(raw, taps, cotangent, decay_rate, rhat, rev, medium_filter)
    grad_residue = res[:, ::per].T * scaled / math.sqrt(float(rows * n * per))
    return mixed, jnp.transpose(grads, (1, 0, 2)), grad_residue


def solution(mesh):
    in_specs = (
        P(("dp", "ctx"), None, "ch"),
        P(None, None, "ch"),
        P("ch", None),
        P("ch", None),
        P("ch", None),
        P(("dp", "ctx"), "ch"),
    )
    out_specs = (P(("dp", "ctx"), "ch"), P(("dp", "ctx"), None, "ch"), P(("dp", "ch"), None))
    return jax.shard_map(
        functools.partial(body, mesh.shape["ctx"]),
        mesh=mesh, in_specs=in_specs, out_specs=out_specs, check_vma=False,
    )
```

```python
import functools
import math

import jax
import jax.numpy as jnp
from jax import lax
from jax.experimental import pallas as pl
from jax.experimental.pallas import tpu as pltpu
from jax.sharding import PartitionSpec as P

F32 = jnp.float32
BF16 = jnp.bfloat16
MESH = pl.DeviceIdType.MESH
B = 128
VMEM_LIMIT = 63 * 2**20


def halves(x):
    hi = x.astype(BF16)
    return hi, (x - hi.astype(F32)).astype(BF16)


def quadrants(a, b, cb):
    out = lax.dot_general(a, b, (((1,), (cb,)), ((), ())), preferred_element_type=F32)
    r, c = out.shape[0] // 2, out.shape[1] // 2
    return (out[:r, :c] + out[:r, c:]) + (out[r:, :c] + out[r:, c:])


def tall(x):
    return jnp.concatenate(halves(x), axis=0)


def flat(x):
    return jnp.concatenate(halves(x), axis=1)


def lanes(shape):
    return lax.broadcasted_iota(jnp.int32, shape, 1)


def rolled(x, shift):
    shift = shift % x.shape[1]
    return pltpu.roll(x, shift, 1) if shift else x


def block_transpose(xs, width):
    count = len(xs)
    chunk = lanes(xs[0].shape) // width
    xs = list(xs)
    bit = 1
    while bit < count:
        high = (chunk & bit) != 0
        for i in range(count):
            if i & bit == 0:
                a, d = xs[i], xs[i | bit]
                xs[i] = jnp.where(high, rolled(d, width * bit), a)
                xs[i | bit] = jnp.where(high, d, rolled(a, -width * bit))
        bit *= 2
    return xs


def kernel(
    n, groups, modes,
    raw_hbm, taps_hbm, cot_hbm, rate_hbm, res_hbm, med_hbm,
    mixed_hbm, grad_hbm, out_hbm,
    mixed_out, grad_out, res_out, ws, taps, rate_ref, residue_ref, med_ref, raw, cot, tf, tb, ls,
    hkv, hq, nq, ncot, ext, feat, hext, qext, yp, yg, head, tail,
    s_all, u_all, msg1, msg2, got1, got2, of, ob, gf, gfr,
    hs, hr, m1s, m1r, m2s, m2r, gs, gr,
):
    rows, chans = cot.shape
    per = chans // groups
    count = rows // B
    short = taps.shape[1]
    loads = [pltpu.make_async_copy(raw_hbm.at[i], raw.at[i], ls.at[i]) for i in range(3)]
    loads.append(pltpu.make_async_copy(cot_hbm, cot, ls.at[3]))
    small_in = ((rate_hbm, rate_ref), (res_hbm, residue_ref), (med_hbm, med_ref), (taps_hbm, taps))
    for i, (src, dst) in enumerate(small_in):
        loads.append(pltpu.make_async_copy(src, dst, ls.at[4 + i]))
    for i in (4, 5, 6, 7, 1, 2, 0, 3):
        loads[i].start()
    me = lax.axis_index("ctx")
    nxt = lax.rem(me + 1, n)
    prv = lax.rem(me + n - 1, n)
    barrier = pltpu.get_barrier_semaphore()
    for k in range(1, n):
        pl.semaphore_signal(
            barrier, inc=1, device_id={"ctx": lax.rem(me + k, n)}, device_id_type=MESH
        )
    pl.semaphore_wait(barrier, n - 1)

    def send(src, dst, ssem, rsem, to):
        copy = pltpu.make_async_remote_copy(
            src_ref=src, dst_ref=dst, send_sem=ssem, recv_sem=rsem,
            device_id={"ctx": to}, device_id_type=MESH,
        )
        copy.start()
        return copy

    halo = [
        send(raw_hbm.at[0:1, rows - 16 : rows], hq, hs.at[0], hr.at[0], nxt),
        send(raw_hbm.at[1:3, rows - 144 : rows], hkv, hs.at[1], hr.at[1], nxt),
        send(raw_hbm.at[0:1, 0:B], nq, hs.at[2], hr.at[2], prv),
        send(cot_hbm.at[0:B], ncot, hs.at[3], hr.at[3], prv),
    ]

    has_prev = jnp.where(me > 0, 1.0, 0.0).astype(F32)
    has_next = jnp.where(me < n - 1, 1.0, 0.0).astype(F32)
    for i in range(4, 8):
        loads[i].wait()
    tap = [[taps[i, k : k + 1, :] for k in range(short)] for i in range(3)]

    def filtered(ref, i, slot, start, size):
        total = tap[i][0] * ref[slot, start : start + size, :]
        for k in range(1, short):
            total = total + tap[i][k] * ref[slot, start - k : start - k + size, :]
        return total

    def expanded(ref):
        tile = jnp.concatenate(
            [jnp.broadcast_to(ref[g : g + 1, :], (modes, modes)) for g in range(groups)], axis=0
        )
        row = lax.broadcasted_iota(jnp.int32, tile.shape, 0) % modes
        column = jnp.sum(jnp.where(lanes(tile.shape) == row, tile, 0.0), axis=1, keepdims=True)
        return jnp.broadcast_to(column, (groups * modes, B))

    rate = expanded(rate_ref)
    twice = 2.0 * rate
    series = 1.0 - twice / 6.0 * (1.0 - twice / 7.0)
    for k in (5.0, 4.0, 3.0, 2.0):
        series = 1.0 - twice / k * series
    scaled = jnp.sqrt(jnp.where(twice < 0.2, twice * series, 1.0 - jnp.exp(-twice)))
    rhat = expanded(residue_ref) * scaled
    lane = lanes(rate.shape)
    lane_f = lane.astype(F32)
    e0 = jnp.exp(-rate * lane_f)
    e2 = jnp.exp(-rate * (B - lane_f))
    e3 = jnp.exp(-rate * (B - 1.0 - lane_f))
    lam = jnp.exp(-rate)
    sub_i = lax.broadcasted_iota(jnp.int32, rate.shape, 0)
    sub_f = sub_i.astype(F32)
    rate_row = jnp.sum(jnp.where(sub_i == lane, rate, 0.0), axis=0, keepdims=True)
    e1t = flat(jnp.exp(-rate_row * (sub_f + 1.0)))
    e2t = flat(jnp.exp(-rate_row * (B - sub_f)))
    square_l, square_s = lane, sub_i

    flip = jnp.where((lane + sub_i) % B == 0, 1.0, 0.0)
    med = med_ref[...]
    med_rev = lax.dot_general(
        med, flip, (((1,), (0,)), ((), ())),
        precision=lax.Precision.HIGHEST, preferred_element_type=F32,
    )
    e_rev = jnp.where(lane == 0, 1.0, e2)

    def band(row):
        return pltpu.roll(jnp.broadcast_to(row, (B, B)), 0, 1, stride=1, stride_axis=0)

    for g in range(groups):
        at = slice(g * modes, (g + 1) * modes)
        hb = jnp.sum(rhat[at] * e0[at], axis=0, keepdims=True)
        hf = jnp.sum(rhat[at] * e_rev[at], axis=0, keepdims=True)
        mb, mf = med[g : g + 1], med_rev[g : g + 1]
        prev = jnp.where(lane > sub_i, band(mf), 0.0)
        cur = jnp.where(lane <= sub_i, band(mf + hf), 0.0)
        tf[g] = tall(jnp.concatenate([prev, cur], axis=1))
        cur = jnp.where(lane >= sub_i, band(mb + hb), 0.0)
        after = jnp.where(lane < sub_i, band(mb), 0.0)
        tb[g] = tall(jnp.concatenate([cur, after], axis=1))

    for i in (1, 2, 0):
        loads[i].wait()
        for j in range(count):
            ext[i, 8 + j * B : 8 + (j + 1) * B, :] = raw[i, j * B : (j + 1) * B, :].astype(F32)
        for j in range(1, count):
            feat[i, j * B : (j + 1) * B, :] = filtered(ext, i, i, 8 + j * B, B)
    loads[3].wait()

    for copy in halo:
        copy.wait()
    ext[0, 0:8, :] = hq[0].astype(F32)[8:16] * has_prev
    for i in (1, 2):
        full = hkv[i - 1].astype(F32) * has_prev
        hext[i - 1] = full
        ext[i, 0:8, :] = full[136:144]
    qext[0, 0:8, :] = ext[0, rows : rows + 8, :]
    qext[0, 8 : 8 + B, :] = nq[0].astype(F32)
    for i in range(3):
        feat[i, 0:B, :] = filtered(ext, i, i, 8, B)
    head[...] = filtered(hext, 1, 0, 16, B) * filtered(hext, 2, 1, 16, B)
    tail[...] = filtered(qext, 0, 0, 8, B) * ncot[...].astype(F32) * has_next

    sub = 16

    def to_groups(t, _):
        products, grads = [], []
        for j in range(count):
            here = pl.ds(pl.multiple_of(j * B + t * sub, sub), sub)
            products.append(feat[1, here, :] * feat[2, here, :])
            grads.append(cot[here, :].astype(F32) * feat[0, here, :])
        there = pl.ds(pl.multiple_of(t * sub, sub), sub)
        for g, y in enumerate(block_transpose(products, per)):
            yp[g, there, :] = y
        for g, y in enumerate(block_transpose(grads, per)):
            yg[g, there, :] = y
        return 0

    lax.fori_loop(0, B // sub, to_groups, 0, unroll=B // sub)

    for g in range(groups):
        at = slice(g * modes, (g + 1) * modes)
        s_all[at, :] = quadrants(tall(e3[at]), flat(yp[g]), 0)
        u_all[at, :] = quadrants(tall(e0[at]), flat(yg[g]), 0)

    state = s_all[...]
    adj = u_all[...]
    u = adj
    step = 1
    while step < count:
        decay = jnp.exp(-rate * float(B * step))
        width = per * step
        state = state + decay * jnp.where(lane >= width, rolled(state, width), 0.0)
        adj = adj + decay * jnp.where(lane < chans - width, rolled(adj, -width), 0.0)
        step *= 2
    starts = jnp.where(lane >= per, rolled(state, per), 0.0)
    ends = jnp.where(lane < chans - per, rolled(adj, -per), 0.0)

    small = lanes((modes, chans)) // per
    final = jnp.zeros((modes, chans), F32)
    first = jnp.zeros((modes, chans), F32)
    for g in range(groups):
        at = slice(g * modes, (g + 1) * modes)
        final = jnp.where(small == g, rolled(state[at], g * per - (count - 1) * per), final)
        first = jnp.where(small == g, rolled(adj[at], g * per), first)
    msg1[0:modes, :] = final
    msg1[modes : 2 * modes, :] = first
    got1[me] = msg1[...]
    sent = []
    for k in range(1, n):
        sent.append(send(msg1, got1.at[me], m1s.at[k], m1r.at[me], lax.rem(me + k, n)))

    up = jnp.exp(rate * lane_f)
    local = lam * starts * u
    terms = jnp.zeros((modes, chans), F32)
    for g in range(groups):
        at = slice(g * modes, (g + 1) * modes)
        cross = quadrants(tall(yg[g]), tall(yp[g]), 1)
        cross = jnp.where(square_s >= square_l, cross, 0.0)
        inner = quadrants(tall(up[at]), tall(cross), 1) * e0[at] + local[at]
        terms = jnp.where(small == g, jnp.sum(inner, axis=1, keepdims=True), terms)
    msg2[...] = terms
    got2[me] = terms
    for k in range(1, n):
        sent.append(send(msg2, got2.at[me], m2s.at[k], m2r.at[me], lax.rem(me + k, n)))

    for g in range(groups):
        cur = yp[g]
        prev = jnp.where(square_l >= per, rolled(cur, per), rolled(head[...], -g * per))
        of[g] = quadrants(tf[g], jnp.concatenate([flat(prev), flat(cur)], axis=0), 0)
        cur = yg[g]
        after = jnp.where(
            square_l < chans - per, rolled(cur, -per), rolled(tail[...], chans - per - g * per)
        )
        ob[g] = quadrants(tb[g], jnp.concatenate([flat(cur), flat(after)], axis=0), 0)

    for k in range(1, n):
        peer = lax.rem(me + k, n)
        pltpu.make_async_remote_copy(
            src_ref=msg1, dst_ref=got1.at[peer], send_sem=m1s.at[k], recv_sem=m1r.at[peer],
            device_id={"ctx": peer}, device_id_type=MESH,
        ).wait_recv()

    rate_c = jnp.zeros((modes, chans), F32)
    for g in range(groups):
        rate_c = jnp.where(small == g, rate[g * modes : (g + 1) * modes], rate_c)
    whole = jnp.exp(-rate_c * float(rows))
    lamc = jnp.exp(-rate_c)
    zero = jnp.zeros((modes, chans), F32)
    run, carry, crossed = zero, zero, zero
    for d in range(n):
        block = got1[d]
        carry = jnp.where(me == d, run, carry)
        crossed = crossed + run * block[modes:]
        run = whole * run + block[:modes]
    run, back = zero, zero
    for d in reversed(range(n)):
        back = jnp.where(me == d, run, back)
        run = whole * run + got1[d][modes:]
    crossed = crossed * lamc

    def spread(x):
        pieces = []
        for g in range(groups):
            pieces.append(jnp.where(small == 0, rolled(x, -g * per), 0.0))
        y = jnp.concatenate(pieces, axis=0)
        width = per
        while width < chans:
            y = y + rolled(y, width)
            width *= 2
        return y

    block_f = (lane // per).astype(F32)
    starts = rhat * (starts + jnp.exp(-rate * (B * block_f)) * spread(carry))
    ends = rhat * (ends + jnp.exp(-rate * (B * (count - 1.0 - block_f))) * spread(back))
    starts = flat(starts)
    ends = flat(ends)

    def carried(table, state, g):
        parts = [state[g * modes : (g + 1) * modes]]
        if g:
            parts.insert(0, jnp.zeros((g * modes, 2 * chans), BF16))
        if g < groups - 1:
            parts.append(jnp.zeros(((groups - 1 - g) * modes, 2 * chans), BF16))
        z = jnp.concatenate(parts, axis=0)
        out = lax.dot_general(
            table, jnp.concatenate([z, z], axis=0), (((1,), (0,)), ((), ())),
            preferred_element_type=F32,
        )
        return out[:, :chans] + out[:, chans:]

    for g in range(groups):
        of[g] = of[g] + carried(e1t, starts, g)
        ob[g] = ob[g] + carried(e2t, ends, g)

    def from_groups(t, _):
        there = pl.ds(pl.multiple_of(t * sub, sub), sub)
        mixed = block_transpose([of[g, there, :] for g in range(groups)], per)
        grads = block_transpose([ob[g, there, :] for g in range(groups)], per)
        for j in range(count):
            here = pl.ds(pl.multiple_of(j * B + t * sub, sub), sub)
            mixed_out[here, :] = (feat[0, here, :] * mixed[j]).astype(BF16)
            gf[0, here, :] = cot[here, :].astype(F32) * mixed[j]
            gf[1, here, :] = grads[j] * feat[2, here, :]
            gf[2, here, :] = grads[j] * feat[1, here, :]
        return 0

    lax.fori_loop(0, B // sub, from_groups, 0, unroll=B // sub)
    writes = []

    def write(src, dst):
        copy = pltpu.make_async_copy(src, dst, ws.at[len(writes)])
        copy.start()
        writes.append(copy)

    last = send(gf.at[:, 0:8], gfr, gs, gr, prv)

    write(mixed_out, mixed_hbm)

    def adjoint(i, start, size):
        total = tap[i][0] * gf[i, start : start + size, :]
        for k in range(1, short):
            total = total + tap[i][k] * gf[i, start + k : start + k + size, :]
        return total

    for i in range(3):
        for j in range(count - 1):
            grad_out[i, j * B : (j + 1) * B, :] = adjoint(i, j * B, B).astype(BF16)
    write(grad_out.at[:, 0 : rows - B], grad_hbm.at[:, 0 : rows - B])
    for k in range(1, n):
        peer = lax.rem(me + k, n)
        pltpu.make_async_remote_copy(
            src_ref=msg2, dst_ref=got2.at[peer], send_sem=m2s.at[k], recv_sem=m2r.at[peer],
            device_id={"ctx": peer}, device_id_type=MESH,
        ).wait_recv()
    total = got2[0]
    for d in range(1, n):
        total = total + got2[d]
    summed = zero
    for g in range(groups):
        part = jnp.sum(jnp.where(small == g, crossed, 0.0), axis=1, keepdims=True)
        summed = jnp.where(small == g, part, summed)
    scale_c = zero
    for g in range(groups):
        scale_c = jnp.where(small == g, scaled[g * modes : (g + 1) * modes], scale_c)
    result = (total + summed) * scale_c * (1.0 / math.sqrt(float(rows * n * per)))
    row = lax.broadcasted_iota(jnp.int32, (modes, chans), 0)
    for g in range(groups):
        first_col = jnp.broadcast_to(rolled(result, -g * per)[:, 0:1], (modes, chans))
        only = jnp.where(row == lanes((modes, chans)), first_col, 0.0)
        res_out[g : g + 1, :] = jnp.sum(only, axis=0, keepdims=True)[:, :modes]
    write(res_out, out_hbm)
    last.wait()
    gf[:, rows : rows + 8, :] = gfr[...] * has_next
    for i in range(3):
        grad_out[i, rows - B : rows, :] = adjoint(i, rows - B, B).astype(BF16)
    write(grad_out.at[:, rows - B : rows], grad_hbm.at[:, rows - B : rows])
    for copy in sent:
        copy.wait_send()
    for copy in writes:
        copy.wait()


def write_out(mixed, grads, res, mixed_hbm, grads_hbm, res_hbm, sems):
    pairs = [(grads.at[i], grads_hbm.at[i]) for i in range(3)]
    pairs += [(mixed, mixed_hbm), (res, res_hbm)]
    copies = [pltpu.make_async_copy(a, b, sems.at[i]) for i, (a, b) in enumerate(pairs)]
    for copy in copies:
        copy.start()
    for copy in copies:
        copy.wait()


def body(n, raw_streams, short_taps, decay_rate, residue, medium_filter, cotangent):
    rows, _, chans = raw_streams.shape
    groups, modes = decay_rate.shape
    per = chans // groups
    raw = jnp.transpose(raw_streams, (1, 0, 2))
    taps = jnp.transpose(short_taps, (1, 0, 2))
    vm = pltpu.VMEM
    dma = pltpu.SemaphoreType.DMA
    hbm = pl.BlockSpec(memory_space=pltpu.HBM)
    shapes = (
        jax.ShapeDtypeStruct((rows, chans), BF16),
        jax.ShapeDtypeStruct((3, rows, chans), BF16),
        jax.ShapeDtypeStruct((groups, modes), F32),
    )
    mixed, grads, res = pl.pallas_call(
        functools.partial(kernel, n, groups, modes),
        out_shape=shapes,
        in_specs=[hbm] * 6,
        out_specs=(hbm, hbm, hbm),
        scratch_shapes=[
            vm((rows, chans), BF16), vm((3, rows, chans), BF16), vm((groups, modes), F32),
            dma((6,)),
            vm(taps.shape, F32), vm(decay_rate.shape, F32), vm(residue.shape, F32),
            vm(medium_filter.shape, F32),
            vm((3, rows, chans), BF16), vm((rows, chans), BF16),
            vm((groups, 2 * B, 2 * B), BF16), vm((groups, 2 * B, 2 * B), BF16), dma((8,)),
            vm((2, 144, chans), BF16), vm((1, 16, chans), BF16),
            vm((1, B, chans), BF16), vm((B, chans), BF16),
            vm((3, rows + 8, chans), F32), vm((3, rows, chans), F32),
            vm((2, 144, chans), F32), vm((1, B + 8, chans), F32),
            vm((groups, B, chans), F32), vm((groups, B, chans), F32),
            vm((B, chans), F32), vm((B, chans), F32),
            vm((groups * modes, chans), F32), vm((groups * modes, chans), F32),
            vm((2 * modes, chans), F32), vm((modes, chans), F32),
            vm((n, 2 * modes, chans), F32), vm((n, modes, chans), F32),
            vm((groups, B, chans), F32), vm((groups, B, chans), F32),
            vm((3, rows + 8, chans), F32), vm((3, 8, chans), F32),
            dma((4,)), dma((4,)), dma((n,)), dma((n,)), dma((n,)), dma((n,)), dma, dma,
        ],
        compiler_params=pltpu.CompilerParams(
            collective_id=0, has_side_effects=True, vmem_limit_bytes=VMEM_LIMIT
        ),
    )(raw, taps, cotangent, decay_rate, residue, medium_filter)
    mixed, grads, res = pl.pallas_call(
        write_out,
        out_shape=shapes,
        in_specs=[hbm] * 3,
        out_specs=(hbm, hbm, hbm),
        scratch_shapes=[dma((5,))],
        compiler_params=pltpu.CompilerParams(has_side_effects=True, vmem_limit_bytes=VMEM_LIMIT),
    )(mixed, grads, res)
    return mixed, jnp.transpose(grads, (1, 0, 2)), res


def solution(mesh):
    in_specs = (
        P(("dp", "ctx"), None, "ch"),
        P(None, None, "ch"),
        P("ch", None),
        P("ch", None),
        P("ch", None),
        P(("dp", "ctx"), "ch"),
    )
    out_specs = (P(("dp", "ctx"), "ch"), P(("dp", "ctx"), None, "ch"), P(("dp", "ch"), None))
    return jax.shard_map(
        functools.partial(body, mesh.shape["ctx"]),
        mesh=mesh, in_specs=in_specs, out_specs=out_specs, check_vma=False,
    )
```

```python
import functools
import math

import jax
import jax.numpy as jnp
from jax import lax
from jax.experimental import pallas as pl
from jax.experimental.pallas import tpu as pltpu
from jax.sharding import PartitionSpec as P

F32 = jnp.float32
BF16 = jnp.bfloat16
MESH = pl.DeviceIdType.MESH
B = 128
VMEM_LIMIT = 63 * 2**20


def halves(x):
    hi = x.astype(BF16)
    return hi, (x - hi.astype(F32)).astype(BF16)


def quadrants(a, b, cb):
    out = lax.dot_general(a, b, (((1,), (cb,)), ((), ())), preferred_element_type=F32)
    r, c = out.shape[0] // 2, out.shape[1] // 2
    return (out[:r, :c] + out[:r, c:]) + (out[r:, :c] + out[r:, c:])


def tall(x):
    return jnp.concatenate(halves(x), axis=0)


def flat(x):
    return jnp.concatenate(halves(x), axis=1)


def lanes(shape):
    return lax.broadcasted_iota(jnp.int32, shape, 1)


def rolled(x, shift):
    shift = shift % x.shape[1]
    return pltpu.roll(x, shift, 1) if shift else x


def block_transpose(xs, width):
    count = len(xs)
    chunk = lanes(xs[0].shape) // width
    xs = list(xs)
    bit = 1
    while bit < count:
        high = (chunk & bit) != 0
        for i in range(count):
            if i & bit == 0:
                a, d = xs[i], xs[i | bit]
                xs[i] = jnp.where(high, rolled(d, width * bit), a)
                xs[i | bit] = jnp.where(high, d, rolled(a, -width * bit))
        bit *= 2
    return xs


def kernel(
    n, groups, modes,
    raw_hbm, taps_hbm, cot_hbm, rate_hbm, res_hbm, med_hbm,
    mixed_hbm, grad_hbm, out_hbm,
    mixed_out, grad_out, res_out, ws, taps, rate_ref, residue_ref, med_ref, raw, cot, tf, tb, ls,
    hkv, hq, nq, ncot, ext, feat, hext, qext, yp, yg, head, tail,
    s_all, u_all, msg1, msg2, got1, got2, of, ob, gf, gfr,
    hs, hr, m1s, m1r, m2s, m2r, gs, gr,
):
    rows, chans = cot.shape
    per = chans // groups
    count = rows // B
    short = taps.shape[1]
    loads = [pltpu.make_async_copy(raw_hbm.at[i], raw.at[i], ls.at[i]) for i in range(3)]
    loads.append(pltpu.make_async_copy(cot_hbm, cot, ls.at[3]))
    small_in = ((rate_hbm, rate_ref), (res_hbm, residue_ref), (med_hbm, med_ref), (taps_hbm, taps))
    for i, (src, dst) in enumerate(small_in):
        loads.append(pltpu.make_async_copy(src, dst, ls.at[4 + i]))
    for i in (4, 5, 6, 7, 1, 2, 0, 3):
        loads[i].start()
    me = lax.axis_index("ctx")
    nxt = lax.rem(me + 1, n)
    prv = lax.rem(me + n - 1, n)
    barrier = pltpu.get_barrier_semaphore()
    for k in range(1, n):
        pl.semaphore_signal(
            barrier, inc=1, device_id={"ctx": lax.rem(me + k, n)}, device_id_type=MESH
        )
    pl.semaphore_wait(barrier, n - 1)

    def send(src, dst, ssem, rsem, to):
        copy = pltpu.make_async_remote_copy(
            src_ref=src, dst_ref=dst, send_sem=ssem, recv_sem=rsem,
            device_id={"ctx": to}, device_id_type=MESH,
        )
        copy.start()
        return copy

    halo = [
        send(raw_hbm.at[0:1, rows - 16 : rows], hq, hs.at[0], hr.at[0], nxt),
        send(raw_hbm.at[1:3, rows - 144 : rows], hkv, hs.at[1], hr.at[1], nxt),
        send(raw_hbm.at[0:1, 0:B], nq, hs.at[2], hr.at[2], prv),
        send(cot_hbm.at[0:B], ncot, hs.at[3], hr.at[3], prv),
    ]

    has_prev = jnp.where(me > 0, 1.0, 0.0).astype(F32)
    has_next = jnp.where(me < n - 1, 1.0, 0.0).astype(F32)
    for i in range(4, 8):
        loads[i].wait()
    tap = [[taps[i, k : k + 1, :] for k in range(short)] for i in range(3)]

    def filtered(ref, i, slot, start, size):
        total = tap[i][0] * ref[slot, start : start + size, :]
        for k in range(1, short):
            total = total + tap[i][k] * ref[slot, start - k : start - k + size, :]
        return total

    def expanded(ref):
        tile = jnp.concatenate(
            [jnp.broadcast_to(ref[g : g + 1, :], (modes, modes)) for g in range(groups)], axis=0
        )
        row = lax.broadcasted_iota(jnp.int32, tile.shape, 0) % modes
        column = jnp.sum(jnp.where(lanes(tile.shape) == row, tile, 0.0), axis=1, keepdims=True)
        return jnp.broadcast_to(column, (groups * modes, B))

    rate = expanded(rate_ref)
    twice = 2.0 * rate
    series = 1.0 - twice / 6.0 * (1.0 - twice / 7.0)
    for k in (5.0, 4.0, 3.0, 2.0):
        series = 1.0 - twice / k * series
    scaled = jnp.sqrt(jnp.where(twice < 0.2, twice * series, 1.0 - jnp.exp(-twice)))
    rhat = expanded(residue_ref) * scaled
    lane = lanes(rate.shape)
    lane_f = lane.astype(F32)
    e0 = jnp.exp(-rate * lane_f)
    e2 = jnp.exp(-rate * (B - lane_f))
    e3 = jnp.exp(-rate * (B - 1.0 - lane_f))
    lam = jnp.exp(-rate)
    sub_i = lax.broadcasted_iota(jnp.int32, rate.shape, 0)
    sub_f = sub_i.astype(F32)
    rate_row = jnp.sum(jnp.where(sub_i == lane, rate, 0.0), axis=0, keepdims=True)
    e1t = flat(jnp.exp(-rate_row * (sub_f + 1.0)))
    e2t = flat(jnp.exp(-rate_row * (B - sub_f)))
    square_l, square_s = lane, sub_i

    flip = jnp.where((lane + sub_i) % B == 0, 1.0, 0.0)
    med = med_ref[...]
    med_rev = lax.dot_general(
        med, flip, (((1,), (0,)), ((), ())),
        precision=lax.Precision.HIGHEST, preferred_element_type=F32,
    )
    e_rev = jnp.where(lane == 0, 1.0, e2)

    def band(row):
        return pltpu.roll(jnp.broadcast_to(row, (B, B)), 0, 1, stride=1, stride_axis=0)

    for g in range(groups):
        at = slice(g * modes, (g + 1) * modes)
        hb = jnp.sum(rhat[at] * e0[at], axis=0, keepdims=True)
        hf = jnp.sum(rhat[at] * e_rev[at], axis=0, keepdims=True)
        mb, mf = med[g : g + 1], med_rev[g : g + 1]
        prev = jnp.where(lane > sub_i, band(mf), 0.0)
        cur = jnp.where(lane <= sub_i, band(mf + hf), 0.0)
        tf[g] = tall(jnp.concatenate([prev, cur], axis=1))
        cur = jnp.where(lane >= sub_i, band(mb + hb), 0.0)
        after = jnp.where(lane < sub_i, band(mb), 0.0)
        tb[g] = tall(jnp.concatenate([cur, after], axis=1))

    for i in (1, 2, 0):
        loads[i].wait()
        for j in range(count):
            ext[i, 8 + j * B : 8 + (j + 1) * B, :] = raw[i, j * B : (j + 1) * B, :].astype(F32)
        for j in range(1, count):
            feat[i, j * B : (j + 1) * B, :] = filtered(ext, i, i, 8 + j * B, B)
    loads[3].wait()

    for copy in halo:
        copy.wait()
    ext[0, 0:8, :] = hq[0].astype(F32)[8:16] * has_prev
    for i in (1, 2):
        full = hkv[i - 1].astype(F32) * has_prev
        hext[i - 1] = full
        ext[i, 0:8, :] = full[136:144]
    qext[0, 0:8, :] = ext[0, rows : rows + 8, :]
    qext[0, 8 : 8 + B, :] = nq[0].astype(F32)
    for i in range(3):
        feat[i, 0:B, :] = filtered(ext, i, i, 8, B)
    head[...] = filtered(hext, 1, 0, 16, B) * filtered(hext, 2, 1, 16, B)
    tail[...] = filtered(qext, 0, 0, 8, B) * ncot[...].astype(F32) * has_next

    sub = 16

    def to_groups(t, _):
        products, grads = [], []
        for j in range(count):
            here = pl.ds(pl.multiple_of(j * B + t * sub, sub), sub)
            products.append(feat[1, here, :] * feat[2, here, :])
            grads.append(cot[here, :].astype(F32) * feat[0, here, :])
        there = pl.ds(pl.multiple_of(t * sub, sub), sub)
        for g, y in enumerate(block_transpose(products, per)):
            yp[g, there, :] = y
        for g, y in enumerate(block_transpose(grads, per)):
            yg[g, there, :] = y
        return 0

    lax.fori_loop(0, B // sub, to_groups, 0, unroll=B // sub)

    for g in range(groups):
        at = slice(g * modes, (g + 1) * modes)
        s_all[at, :] = quadrants(tall(e3[at]), flat(yp[g]), 0)
        u_all[at, :] = quadrants(tall(e0[at]), flat(yg[g]), 0)

    state = s_all[...]
    adj = u_all[...]
    u = adj
    step = 1
    while step < count:
        decay = jnp.exp(-rate * float(B * step))
        width = per * step
        state = state + decay * jnp.where(lane >= width, rolled(state, width), 0.0)
        adj = adj + decay * jnp.where(lane < chans - width, rolled(adj, -width), 0.0)
        step *= 2
    starts = jnp.where(lane >= per, rolled(state, per), 0.0)
    ends = jnp.where(lane < chans - per, rolled(adj, -per), 0.0)

    small = lanes((modes, chans)) // per
    final = jnp.zeros((modes, chans), F32)
    first = jnp.zeros((modes, chans), F32)
    for g in range(groups):
        at = slice(g * modes, (g + 1) * modes)
        final = jnp.where(small == g, rolled(state[at], g * per - (count - 1) * per), final)
        first = jnp.where(small == g, rolled(adj[at], g * per), first)
    msg1[0:modes, :] = final
    msg1[modes : 2 * modes, :] = first
    got1[me] = msg1[...]
    sent = []
    for k in range(1, n):
        sent.append(send(msg1, got1.at[me], m1s.at[k], m1r.at[me], lax.rem(me + k, n)))

    up = jnp.exp(rate * lane_f)
    local = lam * starts * u
    terms = jnp.zeros((modes, chans), F32)
    for g in range(groups):
        at = slice(g * modes, (g + 1) * modes)
        cross = quadrants(tall(yg[g]), tall(yp[g]), 1)
        cross = jnp.where(square_s >= square_l, cross, 0.0)
        inner = quadrants(tall(up[at]), tall(cross), 1) * e0[at] + local[at]
        terms = jnp.where(small == g, jnp.sum(inner, axis=1, keepdims=True), terms)
    msg2[...] = terms
    got2[me] = terms
    for k in range(1, n):
        sent.append(send(msg2, got2.at[me], m2s.at[k], m2r.at[me], lax.rem(me + k, n)))

    for g in range(groups):
        cur = yp[g]
        prev = jnp.where(square_l >= per, rolled(cur, per), rolled(head[...], -g * per))
        of[g] = quadrants(tf[g], jnp.concatenate([flat(prev), flat(cur)], axis=0), 0)
        cur = yg[g]
        after = jnp.where(
            square_l < chans - per, rolled(cur, -per), rolled(tail[...], chans - per - g * per)
        )
        ob[g] = quadrants(tb[g], jnp.concatenate([flat(cur), flat(after)], axis=0), 0)

    for k in range(1, n):
        peer = lax.rem(me + k, n)
        pltpu.make_async_remote_copy(
            src_ref=msg1, dst_ref=got1.at[peer], send_sem=m1s.at[k], recv_sem=m1r.at[peer],
            device_id={"ctx": peer}, device_id_type=MESH,
        ).wait_recv()

    rate_c = jnp.zeros((modes, chans), F32)
    for g in range(groups):
        rate_c = jnp.where(small == g, rate[g * modes : (g + 1) * modes], rate_c)
    whole = jnp.exp(-rate_c * float(rows))
    lamc = jnp.exp(-rate_c)
    zero = jnp.zeros((modes, chans), F32)
    run, carry, crossed = zero, zero, zero
    for d in range(n):
        block = got1[d]
        carry = jnp.where(me == d, run, carry)
        crossed = crossed + run * block[modes:]
        run = whole * run + block[:modes]
    run, back = zero, zero
    for d in reversed(range(n)):
        back = jnp.where(me == d, run, back)
        run = whole * run + got1[d][modes:]
    crossed = crossed * lamc

    def spread(x):
        pieces = []
        for g in range(groups):
            pieces.append(jnp.where(small == 0, rolled(x, -g * per), 0.0))
        y = jnp.concatenate(pieces, axis=0)
        width = per
        while width < chans:
            y = y + rolled(y, width)
            width *= 2
        return y

    block_f = (lane // per).astype(F32)
    starts = rhat * (starts + jnp.exp(-rate * (B * block_f)) * spread(carry))
    ends = rhat * (ends + jnp.exp(-rate * (B * (count - 1.0 - block_f))) * spread(back))
    starts = flat(starts)
    ends = flat(ends)

    def carried(table, state, g):
        parts = [state[g * modes : (g + 1) * modes]]
        if g:
            parts.insert(0, jnp.zeros((g * modes, 2 * chans), BF16))
        if g < groups - 1:
            parts.append(jnp.zeros(((groups - 1 - g) * modes, 2 * chans), BF16))
        z = jnp.concatenate(parts, axis=0)
        out = lax.dot_general(
            table, jnp.concatenate([z, z], axis=0), (((1,), (0,)), ((), ())),
            preferred_element_type=F32,
        )
        return out[:, :chans] + out[:, chans:]

    for g in range(groups):
        of[g] = of[g] + carried(e1t, starts, g)
        ob[g] = ob[g] + carried(e2t, ends, g)

    def from_groups(t, _):
        there = pl.ds(pl.multiple_of(t * sub, sub), sub)
        mixed = block_transpose([of[g, there, :] for g in range(groups)], per)
        grads = block_transpose([ob[g, there, :] for g in range(groups)], per)
        for j in range(count):
            here = pl.ds(pl.multiple_of(j * B + t * sub, sub), sub)
            mixed_out[here, :] = (feat[0, here, :] * mixed[j]).astype(BF16)
            gf[0, here, :] = cot[here, :].astype(F32) * mixed[j]
            gf[1, here, :] = grads[j] * feat[2, here, :]
            gf[2, here, :] = grads[j] * feat[1, here, :]
        return 0

    lax.fori_loop(0, B // sub, from_groups, 0, unroll=B // sub)
    writes = []

    def write(src, dst):
        copy = pltpu.make_async_copy(src, dst, ws.at[len(writes)])
        copy.start()
        writes.append(copy)

    last = send(gf.at[:, 0:8], gfr, gs, gr, prv)

    write(mixed_out, mixed_hbm)

    def adjoint(i, start, size):
        total = tap[i][0] * gf[i, start : start + size, :]
        for k in range(1, short):
            total = total + tap[i][k] * gf[i, start + k : start + k + size, :]
        return total

    for i in range(3):
        for j in range(count - 1):
            grad_out[i, j * B : (j + 1) * B, :] = adjoint(i, j * B, B).astype(BF16)
    write(grad_out.at[:, 0 : rows - B], grad_hbm.at[:, 0 : rows - B])
    for k in range(1, n):
        peer = lax.rem(me + k, n)
        pltpu.make_async_remote_copy(
            src_ref=msg2, dst_ref=got2.at[peer], send_sem=m2s.at[k], recv_sem=m2r.at[peer],
            device_id={"ctx": peer}, device_id_type=MESH,
        ).wait_recv()
    total = got2[0]
    for d in range(1, n):
        total = total + got2[d]
    summed = zero
    for g in range(groups):
        part = jnp.sum(jnp.where(small == g, crossed, 0.0), axis=1, keepdims=True)
        summed = jnp.where(small == g, part, summed)
    scale_c = zero
    for g in range(groups):
        scale_c = jnp.where(small == g, scaled[g * modes : (g + 1) * modes], scale_c)
    result = (total + summed) * scale_c * (1.0 / math.sqrt(float(rows * n * per)))
    row = lax.broadcasted_iota(jnp.int32, (modes, chans), 0)
    for g in range(groups):
        first_col = jnp.broadcast_to(rolled(result, -g * per)[:, 0:1], (modes, chans))
        only = jnp.where(row == lanes((modes, chans)), first_col, 0.0)
        res_out[g : g + 1, :] = jnp.sum(only, axis=0, keepdims=True)[:, :modes]
    write(res_out, out_hbm)
    last.wait()
    gf[:, rows : rows + 8, :] = gfr[...] * has_next
    for i in range(3):
        grad_out[i, rows - B : rows, :] = adjoint(i, rows - B, B).astype(BF16)
    write(grad_out.at[:, rows - B : rows], grad_hbm.at[:, rows - B : rows])
    for copy in sent:
        copy.wait_send()
    for copy in writes:
        copy.wait()


def write_out(mixed, grads, res, mixed_hbm, grads_hbm, res_hbm, m_buf, g_buf, r_buf, ins, outs):
    trips = [(grads.at[i], g_buf.at[i], grads_hbm.at[i]) for i in range(3)]
    trips += [(mixed, m_buf, mixed_hbm), (res, r_buf, res_hbm)]
    reads = [pltpu.make_async_copy(a, b, ins.at[i]) for i, (a, b, c) in enumerate(trips)]
    stores = [pltpu.make_async_copy(b, c, outs.at[i]) for i, (a, b, c) in enumerate(trips)]
    for copy in reads:
        copy.start()
    for read, store in zip(reads, stores):
        read.wait()
        store.start()
    for copy in stores:
        copy.wait()


def body(n, raw_streams, short_taps, decay_rate, residue, medium_filter, cotangent):
    rows, _, chans = raw_streams.shape
    groups, modes = decay_rate.shape
    per = chans // groups
    raw = jnp.transpose(raw_streams, (1, 0, 2))
    taps = jnp.transpose(short_taps, (1, 0, 2))
    vm = pltpu.VMEM
    dma = pltpu.SemaphoreType.DMA
    hbm = pl.BlockSpec(memory_space=pltpu.HBM)
    shapes = (
        jax.ShapeDtypeStruct((rows, chans), BF16),
        jax.ShapeDtypeStruct((3, rows, chans), BF16),
        jax.ShapeDtypeStruct((groups, modes), F32),
    )
    mixed, grads, res = pl.pallas_call(
        functools.partial(kernel, n, groups, modes),
        out_shape=shapes,
        in_specs=[hbm] * 6,
        out_specs=(hbm, hbm, hbm),
        scratch_shapes=[
            vm((rows, chans), BF16), vm((3, rows, chans), BF16), vm((groups, modes), F32),
            dma((6,)),
            vm(taps.shape, F32), vm(decay_rate.shape, F32), vm(residue.shape, F32),
            vm(medium_filter.shape, F32),
            vm((3, rows, chans), BF16), vm((rows, chans), BF16),
            vm((groups, 2 * B, 2 * B), BF16), vm((groups, 2 * B, 2 * B), BF16), dma((8,)),
            vm((2, 144, chans), BF16), vm((1, 16, chans), BF16),
            vm((1, B, chans), BF16), vm((B, chans), BF16),
            vm((3, rows + 8, chans), F32), vm((3, rows, chans), F32),
            vm((2, 144, chans), F32), vm((1, B + 8, chans), F32),
            vm((groups, B, chans), F32), vm((groups, B, chans), F32),
            vm((B, chans), F32), vm((B, chans), F32),
            vm((groups * modes, chans), F32), vm((groups * modes, chans), F32),
            vm((2 * modes, chans), F32), vm((modes, chans), F32),
            vm((n, 2 * modes, chans), F32), vm((n, modes, chans), F32),
            vm((groups, B, chans), F32), vm((groups, B, chans), F32),
            vm((3, rows + 8, chans), F32), vm((3, 8, chans), F32),
            dma((4,)), dma((4,)), dma((n,)), dma((n,)), dma((n,)), dma((n,)), dma, dma,
        ],
        compiler_params=pltpu.CompilerParams(
            collective_id=0, has_side_effects=True, vmem_limit_bytes=VMEM_LIMIT
        ),
    )(raw, taps, cotangent, decay_rate, residue, medium_filter)
    mixed, grads, res = pl.pallas_call(
        write_out,
        out_shape=shapes,
        in_specs=[hbm] * 3,
        out_specs=(hbm, hbm, hbm),
        scratch_shapes=[
            vm((rows, chans), BF16), vm((3, rows, chans), BF16), vm((groups, modes), F32),
            dma((5,)), dma((5,)),
        ],
        compiler_params=pltpu.CompilerParams(has_side_effects=True, vmem_limit_bytes=VMEM_LIMIT),
    )(mixed, grads, res)
    return mixed, jnp.transpose(grads, (1, 0, 2)), res


def solution(mesh):
    in_specs = (
        P(("dp", "ctx"), None, "ch"),
        P(None, None, "ch"),
        P("ch", None),
        P("ch", None),
        P("ch", None),
        P(("dp", "ctx"), "ch"),
    )
    out_specs = (P(("dp", "ctx"), "ch"), P(("dp", "ctx"), None, "ch"), P(("dp", "ch"), None))
    return jax.shard_map(
        functools.partial(body, mesh.shape["ctx"]),
        mesh=mesh, in_specs=in_specs, out_specs=out_specs, check_vma=False,
    )
```

```python
import functools
import math

import jax
import jax.numpy as jnp
from jax import lax
from jax.experimental import pallas as pl
from jax.experimental.pallas import tpu as pltpu
from jax.sharding import PartitionSpec as P

F32 = jnp.float32
BF16 = jnp.bfloat16
MESH = pl.DeviceIdType.MESH
B = 128
VMEM_LIMIT = 64 * 2**20 - 1052672 - 131072


def halves(x):
    hi = x.astype(BF16)
    return hi, (x - hi.astype(F32)).astype(BF16)


def quadrants(a, b, cb):
    out = lax.dot_general(a, b, (((1,), (cb,)), ((), ())), preferred_element_type=F32)
    r, c = out.shape[0] // 2, out.shape[1] // 2
    return (out[:r, :c] + out[:r, c:]) + (out[r:, :c] + out[r:, c:])


def tall(x):
    return jnp.concatenate(halves(x), axis=0)


def flat(x):
    return jnp.concatenate(halves(x), axis=1)


def lanes(shape):
    return lax.broadcasted_iota(jnp.int32, shape, 1)


def rolled(x, shift):
    shift = shift % x.shape[1]
    return pltpu.roll(x, shift, 1) if shift else x


def block_transpose(xs, width):
    count = len(xs)
    chunk = lanes(xs[0].shape) // width
    xs = list(xs)
    bit = 1
    while bit < count:
        high = (chunk & bit) != 0
        for i in range(count):
            if i & bit == 0:
                a, d = xs[i], xs[i | bit]
                xs[i] = jnp.where(high, rolled(d, width * bit), a)
                xs[i | bit] = jnp.where(high, d, rolled(a, -width * bit))
        bit *= 2
    return xs


def kernel(
    n, groups, modes,
    raw_hbm, taps_hbm, cot_hbm, rate_hbm, res_hbm, med_hbm,
    mixed_out, grad_out, res_out, taps, rate_ref, residue_ref, med_ref, raw, cot, tf, tb, ls,
    hkv, hq, nq, ncot, ext, feat, hext, qext, yp, yg, head, tail,
    s_all, u_all, msg1, msg2, got1, got2, of, ob, gf, gfr,
    hs, hr, m1s, m1r, m2s, m2r, gs, gr,
):
    rows, chans = cot.shape
    per = chans // groups
    count = rows // B
    short = taps.shape[1]
    loads = [pltpu.make_async_copy(raw_hbm.at[i], raw.at[i], ls.at[i]) for i in range(3)]
    loads.append(pltpu.make_async_copy(cot_hbm, cot, ls.at[3]))
    small_in = ((rate_hbm, rate_ref), (res_hbm, residue_ref), (med_hbm, med_ref), (taps_hbm, taps))
    for i, (src, dst) in enumerate(small_in):
        loads.append(pltpu.make_async_copy(src, dst, ls.at[4 + i]))
    for i in (4, 5, 6, 7, 1, 2, 0, 3):
        loads[i].start()
    me = lax.axis_index("ctx")
    nxt = lax.rem(me + 1, n)
    prv = lax.rem(me + n - 1, n)
    barrier = pltpu.get_barrier_semaphore()
    for k in range(1, n):
        pl.semaphore_signal(
            barrier, inc=1, device_id={"ctx": lax.rem(me + k, n)}, device_id_type=MESH
        )
    pl.semaphore_wait(barrier, n - 1)

    def send(src, dst, ssem, rsem, to):
        copy = pltpu.make_async_remote_copy(
            src_ref=src, dst_ref=dst, send_sem=ssem, recv_sem=rsem,
            device_id={"ctx": to}, device_id_type=MESH,
        )
        copy.start()
        return copy

    halo = [
        send(raw_hbm.at[0:1, rows - 16 : rows], hq, hs.at[0], hr.at[0], nxt),
        send(raw_hbm.at[1:3, rows - 144 : rows], hkv, hs.at[1], hr.at[1], nxt),
        send(raw_hbm.at[0:1, 0:B], nq, hs.at[2], hr.at[2], prv),
        send(cot_hbm.at[0:B], ncot, hs.at[3], hr.at[3], prv),
    ]

    has_prev = jnp.where(me > 0, 1.0, 0.0).astype(F32)
    has_next = jnp.where(me < n - 1, 1.0, 0.0).astype(F32)
    for i in range(4, 8):
        loads[i].wait()
    tap = [[taps[i, k : k + 1, :] for k in range(short)] for i in range(3)]

    def filtered(ref, i, slot, start, size):
        total = tap[i][0] * ref[slot, start : start + size, :]
        for k in range(1, short):
            total = total + tap[i][k] * ref[slot, start - k : start - k + size, :]
        return total

    def expanded(ref):
        tile = jnp.concatenate(
            [jnp.broadcast_to(ref[g : g + 1, :], (modes, modes)) for g in range(groups)], axis=0
        )
        row = lax.broadcasted_iota(jnp.int32, tile.shape, 0) % modes
        column = jnp.sum(jnp.where(lanes(tile.shape) == row, tile, 0.0), axis=1, keepdims=True)
        return jnp.broadcast_to(column, (groups * modes, B))

    rate = expanded(rate_ref)
    twice = 2.0 * rate
    series = 1.0 - twice / 6.0 * (1.0 - twice / 7.0)
    for k in (5.0, 4.0, 3.0, 2.0):
        series = 1.0 - twice / k * series
    scaled = jnp.sqrt(jnp.where(twice < 0.2, twice * series, 1.0 - jnp.exp(-twice)))
    rhat = expanded(residue_ref) * scaled
    lane = lanes(rate.shape)
    lane_f = lane.astype(F32)
    e0 = jnp.exp(-rate * lane_f)
    e2 = jnp.exp(-rate * (B - lane_f))
    e3 = jnp.exp(-rate * (B - 1.0 - lane_f))
    lam = jnp.exp(-rate)
    sub_i = lax.broadcasted_iota(jnp.int32, rate.shape, 0)
    sub_f = sub_i.astype(F32)
    rate_row = jnp.sum(jnp.where(sub_i == lane, rate, 0.0), axis=0, keepdims=True)
    e1t = flat(jnp.exp(-rate_row * (sub_f + 1.0)))
    e2t = flat(jnp.exp(-rate_row * (B - sub_f)))
    square_l, square_s = lane, sub_i

    flip = jnp.where((lane + sub_i) % B == 0, 1.0, 0.0)
    med = med_ref[...]
    med_rev = lax.dot_general(
        med, flip, (((1,), (0,)), ((), ())),
        precision=lax.Precision.HIGHEST, preferred_element_type=F32,
    )
    e_rev = jnp.where(lane == 0, 1.0, e2)

    def band(row):
        return pltpu.roll(jnp.broadcast_to(row, (B, B)), 0, 1, stride=1, stride_axis=0)

    for g in range(groups):
        at = slice(g * modes, (g + 1) * modes)
        hb = jnp.sum(rhat[at] * e0[at], axis=0, keepdims=True)
        hf = jnp.sum(rhat[at] * e_rev[at], axis=0, keepdims=True)
        mb, mf = med[g : g + 1], med_rev[g : g + 1]
        prev = jnp.where(lane > sub_i, band(mf), 0.0)
        cur = jnp.where(lane <= sub_i, band(mf + hf), 0.0)
        tf[g] = tall(jnp.concatenate([prev, cur], axis=1))
        cur = jnp.where(lane >= sub_i, band(mb + hb), 0.0)
        after = jnp.where(lane < sub_i, band(mb), 0.0)
        tb[g] = tall(jnp.concatenate([cur, after], axis=1))

    for i in (1, 2, 0):
        loads[i].wait()
        for j in range(count):
            ext[i, 8 + j * B : 8 + (j + 1) * B, :] = raw[i, j * B : (j + 1) * B, :].astype(F32)
        for j in range(1, count):
            feat[i, j * B : (j + 1) * B, :] = filtered(ext, i, i, 8 + j * B, B)
    loads[3].wait()

    for copy in halo:
        copy.wait()
    ext[0, 0:8, :] = hq[0].astype(F32)[8:16] * has_prev
    for i in (1, 2):
        full = hkv[i - 1].astype(F32) * has_prev
        hext[i - 1] = full
        ext[i, 0:8, :] = full[136:144]
    qext[0, 0:8, :] = ext[0, rows : rows + 8, :]
    qext[0, 8 : 8 + B, :] = nq[0].astype(F32)
    for i in range(3):
        feat[i, 0:B, :] = filtered(ext, i, i, 8, B)
    head[...] = filtered(hext, 1, 0, 16, B) * filtered(hext, 2, 1, 16, B)
    tail[...] = filtered(qext, 0, 0, 8, B) * ncot[...].astype(F32) * has_next

    sub = 16

    def to_groups(t, _):
        products, grads = [], []
        for j in range(count):
            here = pl.ds(pl.multiple_of(j * B + t * sub, sub), sub)
            products.append(feat[1, here, :] * feat[2, here, :])
            grads.append(cot[here, :].astype(F32) * feat[0, here, :])
        there = pl.ds(pl.multiple_of(t * sub, sub), sub)
        for g, y in enumerate(block_transpose(products, per)):
            yp[g, there, :] = y
        for g, y in enumerate(block_transpose(grads, per)):
            yg[g, there, :] = y
        return 0

    lax.fori_loop(0, B // sub, to_groups, 0, unroll=B // sub)

    for g in range(groups):
        at = slice(g * modes, (g + 1) * modes)
        s_all[at, :] = quadrants(tall(e3[at]), flat(yp[g]), 0)
        u_all[at, :] = quadrants(tall(e0[at]), flat(yg[g]), 0)

    state = s_all[...]
    adj = u_all[...]
    u = adj
    step = 1
    while step < count:
        decay = jnp.exp(-rate * float(B * step))
        width = per * step
        state = state + decay * jnp.where(lane >= width, rolled(state, width), 0.0)
        adj = adj + decay * jnp.where(lane < chans - width, rolled(adj, -width), 0.0)
        step *= 2
    starts = jnp.where(lane >= per, rolled(state, per), 0.0)
    ends = jnp.where(lane < chans - per, rolled(adj, -per), 0.0)

    small = lanes((modes, chans)) // per
    final = jnp.zeros((modes, chans), F32)
    first = jnp.zeros((modes, chans), F32)
    for g in range(groups):
        at = slice(g * modes, (g + 1) * modes)
        final = jnp.where(small == g, rolled(state[at], g * per - (count - 1) * per), final)
        first = jnp.where(small == g, rolled(adj[at], g * per), first)
    msg1[0:modes, :] = final
    msg1[modes : 2 * modes, :] = first
    got1[me] = msg1[...]
    sent = []
    for k in range(1, n):
        sent.append(send(msg1, got1.at[me], m1s.at[k], m1r.at[me], lax.rem(me + k, n)))

    up = jnp.exp(rate * lane_f)
    local = lam * starts * u
    terms = jnp.zeros((modes, chans), F32)
    for g in range(groups):
        at = slice(g * modes, (g + 1) * modes)
        cross = quadrants(tall(yg[g]), tall(yp[g]), 1)
        cross = jnp.where(square_s >= square_l, cross, 0.0)
        inner = quadrants(tall(up[at]), tall(cross), 1) * e0[at] + local[at]
        terms = jnp.where(small == g, jnp.sum(inner, axis=1, keepdims=True), terms)
    msg2[...] = terms
    got2[me] = terms
    for k in range(1, n):
        sent.append(send(msg2, got2.at[me], m2s.at[k], m2r.at[me], lax.rem(me + k, n)))

    for g in range(groups):
        cur = yp[g]
        prev = jnp.where(square_l >= per, rolled(cur, per), rolled(head[...], -g * per))
        of[g] = quadrants(tf[g], jnp.concatenate([flat(prev), flat(cur)], axis=0), 0)
        cur = yg[g]
        after = jnp.where(
            square_l < chans - per, rolled(cur, -per), rolled(tail[...], chans - per - g * per)
        )
        ob[g] = quadrants(tb[g], jnp.concatenate([flat(cur), flat(after)], axis=0), 0)

    for k in range(1, n):
        peer = lax.rem(me + k, n)
        pltpu.make_async_remote_copy(
            src_ref=msg1, dst_ref=got1.at[peer], send_sem=m1s.at[k], recv_sem=m1r.at[peer],
            device_id={"ctx": peer}, device_id_type=MESH,
        ).wait_recv()

    rate_c = jnp.zeros((modes, chans), F32)
    for g in range(groups):
        rate_c = jnp.where(small == g, rate[g * modes : (g + 1) * modes], rate_c)
    whole = jnp.exp(-rate_c * float(rows))
    lamc = jnp.exp(-rate_c)
    zero = jnp.zeros((modes, chans), F32)
    run, carry, crossed = zero, zero, zero
    for d in range(n):
        block = got1[d]
        carry = jnp.where(me == d, run, carry)
        crossed = crossed + run * block[modes:]
        run = whole * run + block[:modes]
    run, back = zero, zero
    for d in reversed(range(n)):
        back = jnp.where(me == d, run, back)
        run = whole * run + got1[d][modes:]
    crossed = crossed * lamc

    def spread(x):
        pieces = []
        for g in range(groups):
            pieces.append(jnp.where(small == 0, rolled(x, -g * per), 0.0))
        y = jnp.concatenate(pieces, axis=0)
        width = per
        while width < chans:
            y = y + rolled(y, width)
            width *= 2
        return y

    block_f = (lane // per).astype(F32)
    starts = rhat * (starts + jnp.exp(-rate * (B * block_f)) * spread(carry))
    ends = rhat * (ends + jnp.exp(-rate * (B * (count - 1.0 - block_f))) * spread(back))
    starts = flat(starts)
    ends = flat(ends)

    def carried(table, state, g):
        parts = [state[g * modes : (g + 1) * modes]]
        if g:
            parts.insert(0, jnp.zeros((g * modes, 2 * chans), BF16))
        if g < groups - 1:
            parts.append(jnp.zeros(((groups - 1 - g) * modes, 2 * chans), BF16))
        z = jnp.concatenate(parts, axis=0)
        out = lax.dot_general(
            table, jnp.concatenate([z, z], axis=0), (((1,), (0,)), ((), ())),
            preferred_element_type=F32,
        )
        return out[:, :chans] + out[:, chans:]

    for g in range(groups):
        of[g] = of[g] + carried(e1t, starts, g)
        ob[g] = ob[g] + carried(e2t, ends, g)

    def from_groups(t, _):
        there = pl.ds(pl.multiple_of(t * sub, sub), sub)
        mixed = block_transpose([of[g, there, :] for g in range(groups)], per)
        grads = block_transpose([ob[g, there, :] for g in range(groups)], per)
        for j in range(count):
            here = pl.ds(pl.multiple_of(j * B + t * sub, sub), sub)
            mixed_out[here, :] = (feat[0, here, :] * mixed[j]).astype(BF16)
            gf[0, here, :] = cot[here, :].astype(F32) * mixed[j]
            gf[1, here, :] = grads[j] * feat[2, here, :]
            gf[2, here, :] = grads[j] * feat[1, here, :]
        return 0

    lax.fori_loop(0, B // sub, from_groups, 0, unroll=B // sub)
    last = send(gf.at[:, 0:8], gfr, gs, gr, prv)

    def adjoint(i, start, size):
        total = tap[i][0] * gf[i, start : start + size, :]
        for k in range(1, short):
            total = total + tap[i][k] * gf[i, start + k : start + k + size, :]
        return total

    for i in range(3):
        for j in range(count - 1):
            grad_out[i, j * B : (j + 1) * B, :] = adjoint(i, j * B, B).astype(BF16)
    for k in range(1, n):
        peer = lax.rem(me + k, n)
        pltpu.make_async_remote_copy(
            src_ref=msg2, dst_ref=got2.at[peer], send_sem=m2s.at[k], recv_sem=m2r.at[peer],
            device_id={"ctx": peer}, device_id_type=MESH,
        ).wait_recv()
    total = got2[0]
    for d in range(1, n):
        total = total + got2[d]
    summed = zero
    for g in range(groups):
        part = jnp.sum(jnp.where(small == g, crossed, 0.0), axis=1, keepdims=True)
        summed = jnp.where(small == g, part, summed)
    scale_c = zero
    for g in range(groups):
        scale_c = jnp.where(small == g, scaled[g * modes : (g + 1) * modes], scale_c)
    result = (total + summed) * scale_c * (1.0 / math.sqrt(float(rows * n * per)))
    row = lax.broadcasted_iota(jnp.int32, (modes, chans), 0)
    for g in range(groups):
        first_col = jnp.broadcast_to(rolled(result, -g * per)[:, 0:1], (modes, chans))
        only = jnp.where(row == lanes((modes, chans)), first_col, 0.0)
        res_out[g : g + 1, :] = jnp.sum(only, axis=0, keepdims=True)[:, :modes]
    last.wait()
    gf[:, rows : rows + 8, :] = gfr[...] * has_next
    for i in range(3):
        grad_out[i, rows - B : rows, :] = adjoint(i, rows - B, B).astype(BF16)
    for copy in sent:
        copy.wait_send()


def write_out(mixed, grads, res, mixed_hbm, grads_hbm, res_hbm, outs):
    trips = [(grads.at[i], grads_hbm.at[i]) for i in range(3)]
    trips += [(mixed, mixed_hbm), (res, res_hbm)]
    stores = [pltpu.make_async_copy(a, b, outs.at[i]) for i, (a, b) in enumerate(trips)]
    for copy in stores:
        copy.start()
    for copy in stores:
        copy.wait()


def body(n, raw_streams, short_taps, decay_rate, residue, medium_filter, cotangent):
    rows, _, chans = raw_streams.shape
    groups, modes = decay_rate.shape
    per = chans // groups
    raw = jnp.transpose(raw_streams, (1, 0, 2))
    taps = jnp.transpose(short_taps, (1, 0, 2))
    vm = pltpu.VMEM
    dma = pltpu.SemaphoreType.DMA
    spec = pl.BlockSpec(memory_space=pltpu.VMEM)
    hbm = pl.BlockSpec(memory_space=pltpu.HBM)
    shapes = (
        jax.ShapeDtypeStruct((rows, chans), BF16),
        jax.ShapeDtypeStruct((3, rows, chans), BF16),
        jax.ShapeDtypeStruct((groups, modes), F32),
    )
    mixed, grads, res = pl.pallas_call(
        functools.partial(kernel, n, groups, modes),
        out_shape=tuple(pltpu.VMEM(x.shape, x.dtype) for x in shapes),
        in_specs=[hbm] * 6,
        out_specs=(spec, spec, spec),
        scratch_shapes=[
            vm(taps.shape, F32), vm(decay_rate.shape, F32), vm(residue.shape, F32),
            vm(medium_filter.shape, F32),
            vm((3, rows, chans), BF16), vm((rows, chans), BF16),
            vm((groups, 2 * B, 2 * B), BF16), vm((groups, 2 * B, 2 * B), BF16), dma((8,)),
            vm((2, 144, chans), BF16), vm((1, 16, chans), BF16),
            vm((1, B, chans), BF16), vm((B, chans), BF16),
            vm((3, rows + 8, chans), F32), vm((3, rows, chans), F32),
            vm((2, 144, chans), F32), vm((1, B + 8, chans), F32),
            vm((groups, B, chans), F32), vm((groups, B, chans), F32),
            vm((B, chans), F32), vm((B, chans), F32),
            vm((groups * modes, chans), F32), vm((groups * modes, chans), F32),
            vm((2 * modes, chans), F32), vm((modes, chans), F32),
            vm((n, 2 * modes, chans), F32), vm((n, modes, chans), F32),
            vm((groups, B, chans), F32), vm((groups, B, chans), F32),
            vm((3, rows + 8, chans), F32), vm((3, 8, chans), F32),
            dma((4,)), dma((4,)), dma((n,)), dma((n,)), dma((n,)), dma((n,)), dma, dma,
        ],
        compiler_params=pltpu.CompilerParams(
            collective_id=0, has_side_effects=True, vmem_limit_bytes=VMEM_LIMIT
        ),
    )(raw, taps, cotangent, decay_rate, residue, medium_filter)
    mixed, grads, res = pl.pallas_call(
        write_out,
        out_shape=shapes,
        in_specs=[spec] * 3,
        out_specs=(hbm, hbm, hbm),
        scratch_shapes=[
            dma((5,)),
        ],
        compiler_params=pltpu.CompilerParams(has_side_effects=True, vmem_limit_bytes=2**20),
    )(mixed, grads, res)
    return mixed, jnp.transpose(grads, (1, 0, 2)), res


def solution(mesh):
    in_specs = (
        P(("dp", "ctx"), None, "ch"),
        P(None, None, "ch"),
        P("ch", None),
        P("ch", None),
        P("ch", None),
        P(("dp", "ctx"), "ch"),
    )
    out_specs = (P(("dp", "ctx"), "ch"), P(("dp", "ctx"), None, "ch"), P(("dp", "ch"), None))
    return jax.shard_map(
        functools.partial(body, mesh.shape["ctx"]),
        mesh=mesh, in_specs=in_specs, out_specs=out_specs, check_vma=False,
    )
```

```python
import functools
import math

import jax
import jax.numpy as jnp
from jax import lax
from jax.experimental import pallas as pl
from jax.experimental.pallas import tpu as pltpu
from jax.sharding import PartitionSpec as P

F32 = jnp.float32
BF16 = jnp.bfloat16
MESH = pl.DeviceIdType.MESH
B = 128
VMEM_LIMIT = 64 * 2**20 - 1052672 - 131072


def halves(x):
    hi = x.astype(BF16)
    return hi, (x - hi.astype(F32)).astype(BF16)


def quadrants(a, b, cb):
    out = lax.dot_general(a, b, (((1,), (cb,)), ((), ())), preferred_element_type=F32)
    r, c = out.shape[0] // 2, out.shape[1] // 2
    return (out[:r, :c] + out[:r, c:]) + (out[r:, :c] + out[r:, c:])


def tall(x):
    return jnp.concatenate(halves(x), axis=0)


def flat(x):
    return jnp.concatenate(halves(x), axis=1)


def lanes(shape):
    return lax.broadcasted_iota(jnp.int32, shape, 1)


def rolled(x, shift):
    shift = shift % x.shape[1]
    return pltpu.roll(x, shift, 1) if shift else x


def block_transpose(xs, width):
    count = len(xs)
    chunk = lanes(xs[0].shape) // width
    xs = list(xs)
    bit = 1
    while bit < count:
        high = (chunk & bit) != 0
        for i in range(count):
            if i & bit == 0:
                a, d = xs[i], xs[i | bit]
                xs[i] = jnp.where(high, rolled(d, width * bit), a)
                xs[i | bit] = jnp.where(high, d, rolled(a, -width * bit))
        bit *= 2
    return xs


def kernel(
    n, groups, modes,
    raw_hbm, taps_hbm, cot_hbm, rate_hbm, res_hbm, med_hbm,
    mixed_out, grad_out, res_out, taps, rate_ref, residue_ref, med_ref, raw, cot, tf, tb, ls,
    hkv, hq, nq, ncot, ext, feat, hext, qext, yp, yg, head, tail,
    s_all, u_all, msg1, msg2, got1, got2, of, ob, gf, gfr,
    hs, hr, m1s, m1r, m2s, m2r, gs, gr,
):
    rows, chans = cot.shape
    per = chans // groups
    count = rows // B
    short = taps.shape[1]
    loads = [pltpu.make_async_copy(raw_hbm.at[i], raw.at[i], ls.at[i]) for i in range(3)]
    loads.append(pltpu.make_async_copy(cot_hbm, cot, ls.at[3]))
    small_in = ((rate_hbm, rate_ref), (res_hbm, residue_ref), (med_hbm, med_ref), (taps_hbm, taps))
    for i, (src, dst) in enumerate(small_in):
        loads.append(pltpu.make_async_copy(src, dst, ls.at[4 + i]))
    for i in (4, 5, 6, 7, 1, 2, 0, 3):
        loads[i].start()
    me = lax.axis_index("ctx")
    nxt = lax.rem(me + 1, n)
    prv = lax.rem(me + n - 1, n)
    barrier = pltpu.get_barrier_semaphore()
    for k in range(1, n):
        pl.semaphore_signal(
            barrier, inc=1, device_id={"ctx": lax.rem(me + k, n)}, device_id_type=MESH
        )
    pl.semaphore_wait(barrier, n - 1)

    def send(src, dst, ssem, rsem, to):
        copy = pltpu.make_async_remote_copy(
            src_ref=src, dst_ref=dst, send_sem=ssem, recv_sem=rsem,
            device_id={"ctx": to}, device_id_type=MESH,
        )
        copy.start()
        return copy

    halo = [
        send(raw_hbm.at[0:1, rows - 16 : rows], hq, hs.at[0], hr.at[0], nxt),
        send(raw_hbm.at[1:3, rows - 144 : rows], hkv, hs.at[1], hr.at[1], nxt),
        send(raw_hbm.at[0:1, 0:B], nq, hs.at[2], hr.at[2], prv),
        send(cot_hbm.at[0:B], ncot, hs.at[3], hr.at[3], prv),
    ]

    has_prev = jnp.where(me > 0, 1.0, 0.0).astype(F32)
    has_next = jnp.where(me < n - 1, 1.0, 0.0).astype(F32)
    for i in range(4, 8):
        loads[i].wait()
    tap = [[taps[i, k : k + 1, :] for k in range(short)] for i in range(3)]

    def filtered(ref, i, slot, start, size):
        total = tap[i][0] * ref[slot, start : start + size, :]
        for k in range(1, short):
            total = total + tap[i][k] * ref[slot, start - k : start - k + size, :]
        return total

    def expanded(ref):
        tile = jnp.concatenate(
            [jnp.broadcast_to(ref[g : g + 1, :], (modes, modes)) for g in range(groups)], axis=0
        )
        row = lax.broadcasted_iota(jnp.int32, tile.shape, 0) % modes
        column = jnp.sum(jnp.where(lanes(tile.shape) == row, tile, 0.0), axis=1, keepdims=True)
        return jnp.broadcast_to(column, (groups * modes, B))

    rate = expanded(rate_ref)
    twice = 2.0 * rate
    series = 1.0 - twice / 6.0 * (1.0 - twice / 7.0)
    for k in (5.0, 4.0, 3.0, 2.0):
        series = 1.0 - twice / k * series
    scaled = jnp.sqrt(jnp.where(twice < 0.2, twice * series, 1.0 - jnp.exp(-twice)))
    rhat = expanded(residue_ref) * scaled
    lane = lanes(rate.shape)
    lane_f = lane.astype(F32)
    e0 = jnp.exp(-rate * lane_f)
    e2 = jnp.exp(-rate * (B - lane_f))
    e3 = jnp.exp(-rate * (B - 1.0 - lane_f))
    lam = jnp.exp(-rate)
    sub_i = lax.broadcasted_iota(jnp.int32, rate.shape, 0)
    sub_f = sub_i.astype(F32)
    rate_row = jnp.sum(jnp.where(sub_i == lane, rate, 0.0), axis=0, keepdims=True)
    e1t = flat(jnp.exp(-rate_row * (sub_f + 1.0)))
    e2t = flat(jnp.exp(-rate_row * (B - sub_f)))
    square_l, square_s = lane, sub_i

    flip = jnp.where((lane + sub_i) % B == 0, 1.0, 0.0)
    med = med_ref[...]
    med_rev = lax.dot_general(
        med, flip, (((1,), (0,)), ((), ())),
        precision=lax.Precision.HIGHEST, preferred_element_type=F32,
    )
    e_rev = jnp.where(lane == 0, 1.0, e2)

    def band(row):
        return pltpu.roll(jnp.broadcast_to(row, (B, B)), 0, 1, stride=1, stride_axis=0)

    for g in range(groups):
        at = slice(g * modes, (g + 1) * modes)
        hb = jnp.sum(rhat[at] * e0[at], axis=0, keepdims=True)
        hf = jnp.sum(rhat[at] * e_rev[at], axis=0, keepdims=True)
        mb, mf = med[g : g + 1], med_rev[g : g + 1]
        prev = jnp.where(lane > sub_i, band(mf), 0.0)
        cur = jnp.where(lane <= sub_i, band(mf + hf), 0.0)
        tf[g] = tall(jnp.concatenate([prev, cur], axis=1))
        cur = jnp.where(lane >= sub_i, band(mb + hb), 0.0)
        after = jnp.where(lane < sub_i, band(mb), 0.0)
        tb[g] = tall(jnp.concatenate([cur, after], axis=1))

    for i in (1, 2, 0):
        loads[i].wait()
        for j in range(count):
            ext[i, 8 + j * B : 8 + (j + 1) * B, :] = raw[i, j * B : (j + 1) * B, :].astype(F32)
        for j in range(1, count):
            feat[i, j * B : (j + 1) * B, :] = filtered(ext, i, i, 8 + j * B, B)
    loads[3].wait()

    for copy in halo:
        copy.wait()
    ext[0, 0:8, :] = hq[0].astype(F32)[8:16] * has_prev
    for i in (1, 2):
        full = hkv[i - 1].astype(F32) * has_prev
        hext[i - 1] = full
        ext[i, 0:8, :] = full[136:144]
    qext[0, 0:8, :] = ext[0, rows : rows + 8, :]
    qext[0, 8 : 8 + B, :] = nq[0].astype(F32)
    for i in range(3):
        feat[i, 0:B, :] = filtered(ext, i, i, 8, B)
    head[...] = filtered(hext, 1, 0, 16, B) * filtered(hext, 2, 1, 16, B)
    tail[...] = filtered(qext, 0, 0, 8, B) * ncot[...].astype(F32) * has_next

    sub = 16

    def to_groups(t, _):
        products, grads = [], []
        for j in range(count):
            here = pl.ds(pl.multiple_of(j * B + t * sub, sub), sub)
            products.append(feat[1, here, :] * feat[2, here, :])
            grads.append(cot[here, :].astype(F32) * feat[0, here, :])
        there = pl.ds(pl.multiple_of(t * sub, sub), sub)
        for g, y in enumerate(block_transpose(products, per)):
            yp[g, there, :] = y
        for g, y in enumerate(block_transpose(grads, per)):
            yg[g, there, :] = y
        return 0

    lax.fori_loop(0, B // sub, to_groups, 0, unroll=B // sub)

    for g in range(groups):
        at = slice(g * modes, (g + 1) * modes)
        s_all[at, :] = quadrants(tall(e3[at]), flat(yp[g]), 0)
        u_all[at, :] = quadrants(tall(e0[at]), flat(yg[g]), 0)

    state = s_all[...]
    adj = u_all[...]
    u = adj
    step = 1
    while step < count:
        decay = jnp.exp(-rate * float(B * step))
        width = per * step
        state = state + decay * jnp.where(lane >= width, rolled(state, width), 0.0)
        adj = adj + decay * jnp.where(lane < chans - width, rolled(adj, -width), 0.0)
        step *= 2
    starts = jnp.where(lane >= per, rolled(state, per), 0.0)
    ends = jnp.where(lane < chans - per, rolled(adj, -per), 0.0)

    small = lanes((modes, chans)) // per
    final = jnp.zeros((modes, chans), F32)
    first = jnp.zeros((modes, chans), F32)
    for g in range(groups):
        at = slice(g * modes, (g + 1) * modes)
        final = jnp.where(small == g, rolled(state[at], g * per - (count - 1) * per), final)
        first = jnp.where(small == g, rolled(adj[at], g * per), first)
    msg1[0:modes, :] = final
    msg1[modes : 2 * modes, :] = first
    got1[me] = msg1[...]
    sent = []
    for k in range(1, n):
        sent.append(send(msg1, got1.at[me], m1s.at[k], m1r.at[me], lax.rem(me + k, n)))

    up = jnp.exp(rate * lane_f)
    local = lam * starts * u
    terms = jnp.zeros((modes, chans), F32)
    for g in range(groups):
        at = slice(g * modes, (g + 1) * modes)
        cross = quadrants(tall(yg[g]), tall(yp[g]), 1)
        cross = jnp.where(square_s >= square_l, cross, 0.0)
        inner = quadrants(tall(up[at]), tall(cross), 1) * e0[at] + local[at]
        terms = jnp.where(small == g, jnp.sum(inner, axis=1, keepdims=True), terms)
    msg2[...] = terms
    got2[me] = terms
    for k in range(1, n):
        sent.append(send(msg2, got2.at[me], m2s.at[k], m2r.at[me], lax.rem(me + k, n)))

    for g in range(groups):
        cur = yp[g]
        prev = jnp.where(square_l >= per, rolled(cur, per), rolled(head[...], -g * per))
        of[g] = quadrants(tf[g], jnp.concatenate([flat(prev), flat(cur)], axis=0), 0)
        cur = yg[g]
        after = jnp.where(
            square_l < chans - per, rolled(cur, -per), rolled(tail[...], chans - per - g * per)
        )
        ob[g] = quadrants(tb[g], jnp.concatenate([flat(cur), flat(after)], axis=0), 0)

    for k in range(1, n):
        peer = lax.rem(me + k, n)
        pltpu.make_async_remote_copy(
            src_ref=msg1, dst_ref=got1.at[peer], send_sem=m1s.at[k], recv_sem=m1r.at[peer],
            device_id={"ctx": peer}, device_id_type=MESH,
        ).wait_recv()

    rate_c = jnp.zeros((modes, chans), F32)
    for g in range(groups):
        rate_c = jnp.where(small == g, rate[g * modes : (g + 1) * modes], rate_c)
    whole = jnp.exp(-rate_c * float(rows))
    lamc = jnp.exp(-rate_c)
    zero = jnp.zeros((modes, chans), F32)
    run, carry, crossed = zero, zero, zero
    for d in range(n):
        block = got1[d]
        carry = jnp.where(me == d, run, carry)
        crossed = crossed + run * block[modes:]
        run = whole * run + block[:modes]
    run, back = zero, zero
    for d in reversed(range(n)):
        back = jnp.where(me == d, run, back)
        run = whole * run + got1[d][modes:]
    crossed = crossed * lamc

    def spread(x):
        pieces = []
        for g in range(groups):
            pieces.append(jnp.where(small == 0, rolled(x, -g * per), 0.0))
        y = jnp.concatenate(pieces, axis=0)
        width = per
        while width < chans:
            y = y + rolled(y, width)
            width *= 2
        return y

    block_f = (lane // per).astype(F32)
    starts = rhat * (starts + jnp.exp(-rate * (B * block_f)) * spread(carry))
    ends = rhat * (ends + jnp.exp(-rate * (B * (count - 1.0 - block_f))) * spread(back))
    starts = flat(starts)
    ends = flat(ends)

    def carried(table, state, g):
        parts = [state[g * modes : (g + 1) * modes]]
        if g:
            parts.insert(0, jnp.zeros((g * modes, 2 * chans), BF16))
        if g < groups - 1:
            parts.append(jnp.zeros(((groups - 1 - g) * modes, 2 * chans), BF16))
        z = jnp.concatenate(parts, axis=0)
        out = lax.dot_general(
            table, jnp.concatenate([z, z], axis=0), (((1,), (0,)), ((), ())),
            preferred_element_type=F32,
        )
        return out[:, :chans] + out[:, chans:]

    for g in range(groups):
        of[g] = of[g] + carried(e1t, starts, g)
        ob[g] = ob[g] + carried(e2t, ends, g)

    def aligned(start):
        return pl.ds(start if isinstance(start, int) else pl.multiple_of(start, sub), sub)

    def from_groups(t, _):
        there = aligned(t * sub)
        mixed = block_transpose([of[g, there, :] for g in range(groups)], per)
        grads = block_transpose([ob[g, there, :] for g in range(groups)], per)
        for j in range(count):
            here = aligned(j * B + t * sub)
            mixed_out[here, :] = (feat[0, here, :] * mixed[j]).astype(BF16)
            gf[0, here, :] = cot[here, :].astype(F32) * mixed[j]
            gf[1, here, :] = grads[j] * feat[2, here, :]
            gf[2, here, :] = grads[j] * feat[1, here, :]
        return 0

    from_groups(0, 0)
    last = send(gf.at[:, 0:8], gfr, gs, gr, prv)
    lax.fori_loop(1, B // sub, from_groups, 0, unroll=B // sub - 1)

    def adjoint(i, start, size):
        total = tap[i][0] * gf[i, start : start + size, :]
        for k in range(1, short):
            total = total + tap[i][k] * gf[i, start + k : start + k + size, :]
        return total

    for i in range(3):
        for j in range(count - 1):
            grad_out[i, j * B : (j + 1) * B, :] = adjoint(i, j * B, B).astype(BF16)
    for k in range(1, n):
        peer = lax.rem(me + k, n)
        pltpu.make_async_remote_copy(
            src_ref=msg2, dst_ref=got2.at[peer], send_sem=m2s.at[k], recv_sem=m2r.at[peer],
            device_id={"ctx": peer}, device_id_type=MESH,
        ).wait_recv()
    total = got2[0]
    for d in range(1, n):
        total = total + got2[d]
    summed = zero
    for g in range(groups):
        part = jnp.sum(jnp.where(small == g, crossed, 0.0), axis=1, keepdims=True)
        summed = jnp.where(small == g, part, summed)
    scale_c = zero
    for g in range(groups):
        scale_c = jnp.where(small == g, scaled[g * modes : (g + 1) * modes], scale_c)
    result = (total + summed) * scale_c * (1.0 / math.sqrt(float(rows * n * per)))
    row = lax.broadcasted_iota(jnp.int32, (modes, chans), 0)
    for g in range(groups):
        first_col = jnp.broadcast_to(rolled(result, -g * per)[:, 0:1], (modes, chans))
        only = jnp.where(row == lanes((modes, chans)), first_col, 0.0)
        res_out[g : g + 1, :] = jnp.sum(only, axis=0, keepdims=True)[:, :modes]
    last.wait()
    gf[:, rows : rows + 8, :] = gfr[...] * has_next
    for i in range(3):
        grad_out[i, rows - B : rows, :] = adjoint(i, rows - B, B).astype(BF16)
    for copy in sent:
        copy.wait_send()


def write_out(mixed, grads, res, mixed_hbm, grads_hbm, res_hbm, outs):
    trips = [(grads.at[i], grads_hbm.at[i]) for i in range(3)]
    trips += [(mixed, mixed_hbm), (res, res_hbm)]
    stores = [pltpu.make_async_copy(a, b, outs.at[i]) for i, (a, b) in enumerate(trips)]
    for copy in stores:
        copy.start()
    for copy in stores:
        copy.wait()


def body(n, raw_streams, short_taps, decay_rate, residue, medium_filter, cotangent):
    rows, _, chans = raw_streams.shape
    groups, modes = decay_rate.shape
    per = chans // groups
    raw = jnp.transpose(raw_streams, (1, 0, 2))
    taps = jnp.transpose(short_taps, (1, 0, 2))
    vm = pltpu.VMEM
    dma = pltpu.SemaphoreType.DMA
    spec = pl.BlockSpec(memory_space=pltpu.VMEM)
    hbm = pl.BlockSpec(memory_space=pltpu.HBM)
    shapes = (
        jax.ShapeDtypeStruct((rows, chans), BF16),
        jax.ShapeDtypeStruct((3, rows, chans), BF16),
        jax.ShapeDtypeStruct((groups, modes), F32),
    )
    mixed, grads, res = pl.pallas_call(
        functools.partial(kernel, n, groups, modes),
        out_shape=tuple(pltpu.VMEM(x.shape, x.dtype) for x in shapes),
        in_specs=[hbm] * 6,
        out_specs=(spec, spec, spec),
        scratch_shapes=[
            vm(taps.shape, F32), vm(decay_rate.shape, F32), vm(residue.shape, F32),
            vm(medium_filter.shape, F32),
            vm((3, rows, chans), BF16), vm((rows, chans), BF16),
            vm((groups, 2 * B, 2 * B), BF16), vm((groups, 2 * B, 2 * B), BF16), dma((8,)),
            vm((2, 144, chans), BF16), vm((1, 16, chans), BF16),
            vm((1, B, chans), BF16), vm((B, chans), BF16),
            vm((3, rows + 8, chans), F32), vm((3, rows, chans), F32),
            vm((2, 144, chans), F32), vm((1, B + 8, chans), F32),
            vm((groups, B, chans), F32), vm((groups, B, chans), F32),
            vm((B, chans), F32), vm((B, chans), F32),
            vm((groups * modes, chans), F32), vm((groups * modes, chans), F32),
            vm((2 * modes, chans), F32), vm((modes, chans), F32),
            vm((n, 2 * modes, chans), F32), vm((n, modes, chans), F32),
            vm((groups, B, chans), F32), vm((groups, B, chans), F32),
            vm((3, rows + 8, chans), F32), vm((3, 8, chans), F32),
            dma((4,)), dma((4,)), dma((n,)), dma((n,)), dma((n,)), dma((n,)), dma, dma,
        ],
        compiler_params=pltpu.CompilerParams(
            collective_id=0, has_side_effects=True, vmem_limit_bytes=VMEM_LIMIT
        ),
    )(raw, taps, cotangent, decay_rate, residue, medium_filter)
    mixed, grads, res = pl.pallas_call(
        write_out,
        out_shape=shapes,
        in_specs=[spec] * 3,
        out_specs=(hbm, hbm, hbm),
        scratch_shapes=[
            dma((5,)),
        ],
        compiler_params=pltpu.CompilerParams(has_side_effects=True, vmem_limit_bytes=2**20),
    )(mixed, grads, res)
    return mixed, jnp.transpose(grads, (1, 0, 2)), res


def solution(mesh):
    in_specs = (
        P(("dp", "ctx"), None, "ch"),
        P(None, None, "ch"),
        P("ch", None),
        P("ch", None),
        P("ch", None),
        P(("dp", "ctx"), "ch"),
    )
    out_specs = (P(("dp", "ctx"), "ch"), P(("dp", "ctx"), None, "ch"), P(("dp", "ch"), None))
    return jax.shard_map(
        functools.partial(body, mesh.shape["ctx"]),
        mesh=mesh, in_specs=in_specs, out_specs=out_specs, check_vma=False,
    )
```
